128 devices in a mesh: row: 16 (over x_lo, y, core), col: 8 (over z, x_hi).
Axes of the slice: x: 4 (x_hi: 2, x_lo: 2; x = x_hi * 2 + x_lo), y: 4, z: 4, core: 2. Of those that a mesh axis runs over, the one named last changes fastest.
Arguments:
- residual: float32 [16, 2048, 128], P(None, 'row'), may hold values from -6 to 6
- diag_inverse: bfloat16 [2, 2048, 2048], P(None, 'col', 'row'), as said below
- panels: bfloat16 [2, 16, 2048, 2048], P(None, None, 'row', 'col'), may hold values from -0.125 to 0.125
- first_block: int32 [1], replicated, may hold values from 0 to 14
- probe_solved: bfloat16 [16, 2048, 128], P(None, 'row'), may hold values from -6 to 6
- genotypes: bfloat16 [16, 2048, 16384], P(None, 'row', 'col'), may hold values from -6 to 6
- annotation: int32 [16384], P('col'), may hold values from 0 to 7
Outputs:
- trailing: float32 [16, 2048, 128], P(None, 'row')
- solved: float32 [2, 2048, 128], P(None, 'col')
- grm_products: bfloat16 [16, 2048, 8, 128], P(None, 'row', 'col')
The draws below stay inside these ranges and needn't reach their ends.
Inputs may be any that keep to these rules, and one draw needn't show every extreme that they name: The two solve steps are blocks first_block and first_block + 1. diag_inverse is lower triangular in each of its two blocks.
All inputs are finite; a program needn't handle non-finite values.
Results may differ from the reference program's by a relative error of at most 0.0085.
Values may be sent and summed in bfloat16 or wider, within the bound.
A program may use at most 128 MiB of HBM per device.

```python
import jax
import jax.numpy as jnp
from jax import lax

B = 2048
R = 128
A = 8
SNPS = 16384
NBLK = 16


def draw_diag_inverse(key, part):
    key_off, key_diag = jax.random.split(key)
    rows_idx = lax.broadcasted_iota(jnp.int32, (2, B, B), 1)
    cols_idx = lax.broadcasted_iota(jnp.int32, (2, B, B), 2)
    off_part = jax.random.normal(key_off, (2, B, B), jnp.float32) / jnp.sqrt(jnp.float32(B))
    diag_part = jax.random.uniform(key_diag, (2, B, B), jnp.float32, 0.7, 1.3)
    lower = jnp.where(rows_idx > cols_idx, off_part, jnp.where(rows_idx == cols_idx, diag_part, 0.0))
    return lower.astype(jnp.bfloat16)


def place_ends(drawn, own_key, smallest, top_value):
    dims = drawn.shape
    spot = [jax.random.randint(jax.random.fold_in(own_key, axis), (), 0, dims[axis]) for axis in range(len(dims))]
    drawn = drawn.at[tuple(spot)].set(smallest)
    longest = dims.index(max(dims))
    spot[longest] = (spot[longest] + 1) % dims[longest]
    return drawn.at[tuple(spot)].set(top_value)


def level_of(key, dims, cuts, low, high):
    factor_of, own = 1.0, jax.random.fold_in(key, 6)
    for dim, shards_of in cuts:
        draws = jnp.exp(jax.random.uniform(jax.random.fold_in(own, dim), (shards_of,), jnp.float32, low / len(cuts), high / len(cuts)))
        factor_of = factor_of * jnp.repeat(draws, dims[dim] // shards_of).reshape([-1 if axis == dim else 1 for axis in range(len(dims))])
    return factor_of


def scatter_about(stream_key, dims, spread, most, shards=(), held_as=jnp.bfloat16):
    drawn = spread * jax.random.normal(stream_key, dims, jnp.float32)
    if shards:
        drawn = drawn * level_of(stream_key, dims, shards, -0.22, 0.18)
    return jnp.clip(drawn, -most, most).astype(held_as)


def setup_inputs(seed: int = 0) -> dict:
    arg_keys = jax.random.split(jax.random.key(seed), 8)
    return {
        "residual": scatter_about(arg_keys[0], (NBLK, B, R), 1.0, 6.0, ((1, 16),), jnp.float32),
        "diag_inverse": draw_diag_inverse(jax.random.fold_in(arg_keys[7], 71), 0),
        "panels": scatter_about(arg_keys[2], (2, NBLK, B, B), B ** -0.5, 0.125, ((2, 16), (3, 8))),
        "first_block": jax.random.randint(arg_keys[3], (1,), 0, NBLK - 1).astype(jnp.int32),
        "probe_solved": scatter_about(arg_keys[4], (NBLK, B, R), 1.0, 6.0, ((1, 16),)),
        "genotypes": scatter_about(arg_keys[5], (NBLK, B, SNPS), 1.0, 6.0, ((1, 16), (2, 8))),
        "annotation": place_ends(jax.random.randint(arg_keys[6], (SNPS,), 0, A), jax.random.fold_in(arg_keys[6], 1), 0, A - 1).astype(jnp.int32),
    }


def reference(residual, diag_inverse, panels, first_block, probe_solved, genotypes, annotation):
    block_now = first_block[0].astype(jnp.int32)
    positions = jnp.arange(NBLK, dtype=jnp.int32)
    current = residual
    solved_list = []
    for section in range(2):
        target = block_now + section
        row_values = lax.dynamic_index_in_dim(current, target, 0, keepdims=False)
        solved_now = jnp.dot(diag_inverse[section], row_values.astype(jnp.bfloat16), preferred_element_type=jnp.float32)
        update = jnp.dot(panels[section].reshape(NBLK * B, B), solved_now.astype(jnp.bfloat16), preferred_element_type=jnp.float32).reshape(NBLK, B, R)
        keep_mask = (positions > target).astype(jnp.float32)[:, None, None]
        current = current - keep_mask * update
        solved_list.append(solved_now)
    flat_geno = genotypes.reshape(NBLK * B, SNPS)
    loadings = jnp.dot(flat_geno.T, probe_solved.reshape(NBLK * B, R), preferred_element_type=jnp.float32)
    rounded = (loadings * (1.0 / SNPS)).astype(jnp.bfloat16)
    onehot = annotation[:, None] == jnp.arange(A, dtype=jnp.int32)[None, :]
    weights = jnp.where(onehot[:, :, None], rounded[:, None, :], jnp.zeros((), jnp.bfloat16)).reshape(SNPS, A * R)
    grm_products = jnp.dot(flat_geno, weights, preferred_element_type=jnp.float32).reshape(NBLK, B, A, R).astype(jnp.bfloat16)
    return current, jnp.stack(solved_list), grm_products
```

```python
import jax
import jax.numpy as jnp
from jax import lax
from jax.experimental import pallas as pl
from jax.experimental.pallas import tpu as pltpu
from jax.sharding import PartitionSpec as P

MESH = pl.DeviceIdType.MESH
F32 = jnp.float32
BF16 = jnp.bfloat16
SNPS = 16384
CHIPS = 8
COLS = 8
UNIT = 512


def dot(a, b):
    return jnp.dot(a, b, preferred_element_type=F32)


def dot_nt(a, b):
    return lax.dot_general(a, b, (((1,), (1,)), ((), ())), preferred_element_type=F32)


def kernel(
    first_ref, residual, diag, panels, probe, geno, annot,
    trailing, solved, grm,
    res_v, diag_v, pan_v, probe_v, pt_v, geno_v, ann_v,
    half_s, core_r, chip_r, full_s, full_r,
    u_r, t0_v, t_s, t_r, upd_v,
    lo_s, lo_r, l_s, l_r, lf_v, lfo_v, w_v,
    za_s, za_r, zd_s, zc_s, zb_r, xs_s, xs_r, xown_v, c0_v, zx_s, zx_r,
    xa_s, xa_r, xd_s, xc_s, xb_r, out_v, sol_v, trail_v,
    in_sem, geno_sem, out_sem,
    core_sem, chip_sem, full_sem, u_sem, t_sem, upd_sem,
    lo_sem, l_sem, lf_sem, lfo_sem, za_sem, zb_sem, xs_sem, zx_sem, xa_sem, xb_sem,
):
    row, col = lax.axis_index("row"), lax.axis_index("col")
    chip, core = lax.div(row, 2), lax.rem(row, 2)
    zpos, xhi = lax.div(col, 2), lax.rem(col, 2)

    def mate():
        return (chip * 2 + (1 - core), col)

    def chip_at(offset):
        return (lax.rem(chip + offset, CHIPS) * 2 + core, col)

    def col_at(offset):
        return (row, lax.rem(col + offset, COLS))

    def z_at(offset):
        return (row, lax.rem(zpos + offset, 4) * 2 + xhi)

    def x_mate():
        return (row, zpos * 2 + (1 - xhi))

    pending = []

    def remote(src, dst, sems, index, to):
        copy = pltpu.make_async_remote_copy(
            src_ref=src, dst_ref=dst, send_sem=sems.at[0, index], recv_sem=sems.at[1, index],
            device_id=to, device_id_type=MESH,
        )
        return copy

    def send(src, dst, sems, index, to):
        copy = remote(src, dst, sems, index, to)
        copy.start()
        pending.append(copy)
        return copy

    def local(src, dst, sem):
        copy = pltpu.make_async_copy(src, dst, sem)
        copy.start()
        return copy

    c_res = local(residual, res_v, in_sem.at[0])
    c_diag = local(diag, diag_v, in_sem.at[1])
    c_probe = local(probe, probe_v, in_sem.at[2])
    c_geno = []
    for g in range(8):
        base = (1 - core) * 1024 if g < 4 else core * 1024
        start = pl.multiple_of(base + (g % 4) * 256, 256)
        c_geno.append(local(geno.at[:, pl.ds(start, 256)], geno_v.at[:, pl.ds(g * 256, 256)], geno_sem.at[g]))
    c_pan = local(panels, pan_v, in_sem.at[3])
    other8 = pl.multiple_of((1 - core) * 8, 8)
    own8 = pl.multiple_of(core * 8, 8)
    c_ann0 = local(annot.at[pl.ds(other8, 8)], ann_v.at[pl.ds(0, 8)], in_sem.at[4])
    c_ann1 = local(annot.at[pl.ds(own8, 8)], ann_v.at[pl.ds(8, 8)], in_sem.at[5])

    barrier = pltpu.get_barrier_semaphore()
    pl.semaphore_signal(barrier, inc=1, device_id=mate(), device_id_type=MESH)
    for d in range(1, CHIPS):
        pl.semaphore_signal(barrier, inc=1, device_id=chip_at(d), device_id_type=MESH)
    for d in range(1, COLS):
        pl.semaphore_signal(barrier, inc=1, device_id=col_at(d), device_id_type=MESH)

    block = first_ref[0]

    def solve_begin(s, values):
        partial = dot(diag_v[s], values.astype(BF16))
        half_s[s, 0] = partial[:128]
        half_s[s, 1] = partial[128:]

    def solve_core(s):
        send(half_s.at[s, 1 - core], core_r.at[s], core_sem, s, mate())

    def solve_chips(s):
        remote(core_r.at[s], core_r.at[s], core_sem, s, mate()).wait_recv()
        chip_r[s, chip] = (half_s[s, core] + core_r[s]).astype(BF16)
        for d in range(1, CHIPS):
            send(chip_r.at[s, chip], chip_r.at[s, chip], chip_sem, s * 8 + d, chip_at(d))

    def solve_sum(s):
        for d in range(1, CHIPS):
            slot = lax.rem(chip + CHIPS - d, CHIPS)
            remote(chip_r.at[s, slot], chip_r.at[s, slot], chip_sem, s * 8 + d, chip_at(d)).wait_recv()
        total = chip_r[s, 0].astype(F32)
        for p in range(1, CHIPS):
            total = total + chip_r[s, p].astype(F32)
        full_s[s] = total
        send(full_s.at[s], full_r.at[s], full_sem, s, mate())

    def solve_end(s):
        remote(full_s.at[s], full_r.at[s], full_sem, s, mate()).wait_recv()
        sol_v[s, core] = full_s[s]
        sol_v[s, 1 - core] = full_r[s]
        return jnp.concatenate([sol_v[s, 0], sol_v[s, 1]], axis=0).astype(BF16)

    c_res.wait()
    c_diag.wait()
    solve_begin(0, res_v[block])
    c_probe.wait()
    pt_v[...] = probe_v[...].T

    for g in range(4):
        c_geno[g].wait()
        part = dot(pt_v[...], geno_v[:, pl.ds(g * 256, 256)]).astype(BF16)
        lo_s[g, :, :] = part
        if g == 0:
            pl.semaphore_wait(barrier, 15)
            solve_core(0)
        send(lo_s.at[g], lo_r.at[g], lo_sem, g, mate())
        if g == 1:
            solve_chips(0)
    for g in range(4):
        c_geno[4 + g].wait()
        part = dot(pt_v[...], geno_v[:, pl.ds((4 + g) * 256, 256)])
        remote(lo_s.at[g], lo_r.at[g], lo_sem, g, mate()).wait_recv()
        part = (part + lo_r[g].astype(F32)).astype(BF16)
        for h in range(2):
            p = 2 * g + h
            l_s[p] = part[:, h * 128:(h + 1) * 128]

            @pl.when(chip != p)
            def _():
                d = lax.rem(p + CHIPS - chip, CHIPS)
                remote(l_s.at[p], l_r.at[d], l_sem, d, (p * 2 + core, col)).start()

    solve_sum(0)

    total = l_s[chip].astype(F32)
    for d in range(1, CHIPS):
        remote(l_s.at[0], l_r.at[d], l_sem, d, chip_at(d)).wait_recv()
        total = total + l_r[d].astype(F32)
    lf_v[chip] = (total * (1.0 / SNPS)).astype(BF16)
    for d in range(1, CHIPS):
        send(lf_v.at[chip], lf_v.at[chip], lf_sem, d, chip_at(d))
    send(lf_v.at[chip], lfo_v.at[chip], lfo_sem, 0, mate())

    solved0 = solve_end(0)
    c_pan.wait()
    u_r[col] = dot(pan_v[0, block + 1], solved0).astype(BF16)
    for d in range(1, COLS):
        send(u_r.at[col], u_r.at[col], u_sem, d, col_at(d))
    for j in range(COLS):
        for h in range(2):
            b = 2 * j + h
            keep = jnp.where(b > block, 1.0, 0.0).astype(F32)
            t0_v[j, h * 128:(h + 1) * 128] = dot(pan_v[0, b], solved0) * keep

    for d in range(1, CHIPS):
        slot = lax.rem(chip + CHIPS - d, CHIPS)
        remote(lf_v.at[slot], lf_v.at[slot], lf_sem, d, chip_at(d)).wait_recv()
        send(lf_v.at[slot], lfo_v.at[slot], lfo_sem, d, mate())

    z_off = (2, 1, 3, 0)
    c_ann0.wait()
    c_ann1.wait()

    def build(chunk, value):
        ids = ann_v[pl.ds(chunk, 1), :]
        for s in range(4):
            for side in range(2):
                owner = lax.rem(zpos + z_off[s], 4) * 2 + (xhi if side == 0 else 1 - xhi)
                mask = jnp.where(ids == owner, 1.0, 0.0).astype(BF16)
                w_v[s, side * 128:(side + 1) * 128, chunk * 128:(chunk + 1) * 128] = value * mask

    for p in range(CHIPS):
        build(8 + p, lf_v[p])
    for d in range(CHIPS):
        slot = lax.rem(chip + CHIPS - d, CHIPS)
        remote(lf_v.at[slot], lfo_v.at[slot], lfo_sem, d, mate()).wait_recv()
    for p in range(CHIPS):
        build(p, lfo_v[p])

    def unit(b, s):
        return dot_nt(geno_v[pl.ds(b * UNIT, UNIT), :], w_v[s])

    Z2, ZP, ZM, Z0 = 0, 1, 2, 3

    def x_first(b, s):
        value = unit(2 + b, s)
        xown_v[b, s] = value[:, :128]
        xs_s[b, s] = value[:, 128:].astype(BF16)
        send(xs_s.at[b, s], xs_r.at[b, s], xs_sem, b * 4 + s, x_mate())

    def x_arrived(b, s):
        remote(xs_s.at[b, s], xs_r.at[b, s], xs_sem, b * 4 + s, x_mate()).wait_recv()
        return xown_v[b, s] + xs_r[b, s].astype(F32)

    za_s[0] = unit(0, Z2).astype(BF16)
    send(za_s.at[0], za_r.at[0], za_sem, 0, z_at(1))
    za_s[1] = unit(1, Z2).astype(BF16)
    send(za_s.at[1], za_r.at[1], za_sem, 1, z_at(3))
    x_first(0, Z2)

    for d in range(1, COLS):
        slot = lax.rem(col + COLS - d, COLS)
        remote(u_r.at[slot], u_r.at[slot], u_sem, d, col_at(d)).wait_recv()
    u_total = u_r[0].astype(F32)
    for j in range(1, COLS):
        u_total = u_total + u_r[j].astype(F32)
    solve_begin(1, res_v[block + 1] - u_total)
    solve_core(1)

    x_first(1, Z2)
    solve_chips(1)

    zd_s[0] = unit(1, ZP).astype(BF16)
    send(zd_s.at[0], zb_r.at[0, 1], zb_sem, 1, z_at(1))
    zd_s[1] = unit(0, ZM).astype(BF16)
    send(zd_s.at[1], zb_r.at[1, 0], zb_sem, 2, z_at(3))
    x_first(0, ZP)
    x_first(1, ZP)
    solve_sum(1)
    x_first(0, ZM)
    solved1 = solve_end(1)
    for j in range(COLS):
        for h in range(2):
            b = 2 * j + h
            keep = jnp.where(b > block + 1, 1.0, 0.0).astype(F32)
            rows = pl.ds(h * 128, 128)
            t_s[j, rows] = (t0_v[j, rows] + dot(pan_v[1, b], solved1) * keep).astype(BF16)
    for d in range(1, COLS):
        to = lax.rem(col + d, COLS)
        send(t_s.at[to], t_r.at[d], t_sem, d, (row, to))
    x_first(1, ZM)

    value = unit(0, ZP)
    remote(za_s.at[0], za_r.at[0], za_sem, 0, z_at(1)).wait_recv()
    zc_s[0] = (value + za_r[0].astype(F32)).astype(BF16)
    send(zc_s.at[0], zb_r.at[0, 0], zb_sem, 0, z_at(1))
    value = unit(1, ZM)
    remote(za_s.at[1], za_r.at[1], za_sem, 1, z_at(3)).wait_recv()
    zc_s[1] = (value + za_r[1].astype(F32)).astype(BF16)
    send(zc_s.at[1], zb_r.at[1, 1], zb_sem, 3, z_at(3))

    x_first(0, Z0)
    x_first(1, Z0)

    xa_s[0] = x_arrived(0, Z2).astype(BF16)
    send(xa_s.at[0], xa_r.at[0], xa_sem, 0, z_at(1))
    xa_s[1] = x_arrived(1, Z2).astype(BF16)
    send(xa_s.at[1], xa_r.at[1], xa_sem, 1, z_at(3))
    xd_s[0] = x_arrived(1, ZP).astype(BF16)
    send(xd_s.at[0], xb_r.at[0, 1], xb_sem, 1, z_at(1))
    xd_s[1] = x_arrived(0, ZM).astype(BF16)
    send(xd_s.at[1], xb_r.at[1, 0], xb_sem, 2, z_at(3))

    total = t_s[col].astype(F32)
    for d in range(1, COLS):
        remote(t_s.at[0], t_r.at[d], t_sem, d, col_at(d)).wait_recv()
        total = total + t_r[d].astype(F32)
    upd_v[col] = total.astype(BF16)
    for d in range(1, COLS):
        send(upd_v.at[col], upd_v.at[col], upd_sem, d, col_at(d))

    c0_v[0] = unit(0, Z0)
    c0_v[1] = unit(1, Z0)

    def z_arrived(b):
        for way in range(2):
            remote(zc_s.at[0], zb_r.at[way, b], zb_sem, way * 2 + b, z_at(1)).wait_recv()
        sums = c0_v[b] + zb_r[0, b].astype(F32) + zb_r[1, b].astype(F32)
        c0_v[b] = sums
        zx_s[b] = sums[:, 128:].astype(BF16)
        send(zx_s.at[b], zx_r.at[b], zx_sem, b, x_mate())

    z_arrived(1)
    z_arrived(0)

    value = x_arrived(0, ZP)
    remote(xa_s.at[0], xa_r.at[0], xa_sem, 0, z_at(1)).wait_recv()
    xc_s[0] = (value + xa_r[0].astype(F32)).astype(BF16)
    send(xc_s.at[0], xb_r.at[0, 0], xb_sem, 0, z_at(1))
    value = x_arrived(1, ZM)
    remote(xa_s.at[1], xa_r.at[1], xa_sem, 1, z_at(3)).wait_recv()
    xc_s[1] = (value + xa_r[1].astype(F32)).astype(BF16)
    send(xc_s.at[1], xb_r.at[1, 1], xb_sem, 3, z_at(3))

    outs = [local(sol_v, solved, out_sem.at[0])]

    for d in range(1, COLS):
        slot = lax.rem(col + COLS - d, COLS)
        remote(upd_v.at[slot], upd_v.at[slot], upd_sem, d, col_at(d)).wait_recv()
    for j in range(COLS):
        for h in range(2):
            rows = pl.ds(h * 128, 128)
            trail_v[2 * j + h] = res_v[2 * j + h] - upd_v[j, rows].astype(F32)
    outs.append(local(trail_v, trailing, out_sem.at[1]))

    def emit(b, value):
        rows = pl.ds(b * UNIT, UNIT)
        out_v[rows, :] = value.astype(BF16)
        outs.append(local(out_v.at[rows], grm.at[rows], out_sem.at[2 + b]))

    for b in range(2):
        remote(zx_s.at[b], zx_r.at[b], zx_sem, b, x_mate()).wait_recv()
        emit(b, c0_v[b, :, :128] + zx_r[b].astype(F32))
    for b in range(2):
        value = x_arrived(b, Z0)
        for way in range(2):
            remote(xc_s.at[0], xb_r.at[way, b], xb_sem, way * 2 + b, z_at(1)).wait_recv()
            value = value + xb_r[way, b].astype(F32)
        emit(2 + b, value)

    for copy in pending:
        copy.wait_send()
    for d in range(1, CHIPS):
        remote(l_s.at[0], l_r.at[d], l_sem, d, chip_at(d)).wait_send()
    for copy in outs:
        copy.wait()


def shards(residual, diag_inverse, panels, first_block, probe_solved, genotypes, annotation):
    blocks, per_row, rhs = residual.shape
    rows = blocks * per_row
    snps = genotypes.shape[2]
    vmem = pltpu.VMEM
    sem = pltpu.SemaphoreType.DMA
    anywhere = pl.BlockSpec(memory_space=pl.ANY)
    scratch = [
        vmem((16, 128, 128), F32), vmem((2, 256, 128), BF16), vmem((2, 16, 128, 256), BF16),
        vmem((rows, rhs), BF16), vmem((rhs, rows), BF16), vmem((rows, snps), BF16), vmem((16, 128), jnp.int32),
        vmem((2, 2, 128, 128), F32), vmem((2, 128, 128), F32), vmem((2, 8, 128, 128), BF16),
        vmem((2, 128, 128), F32), vmem((2, 128, 128), F32),
        vmem((8, 128, 128), BF16), vmem((8, 256, 128), F32), vmem((8, 256, 128), BF16), vmem((8, 256, 128), BF16),
        vmem((8, 256, 128), BF16),
        vmem((4, 128, 256), BF16), vmem((4, 128, 256), BF16), vmem((8, 128, 128), BF16), vmem((8, 128, 128), BF16),
        vmem((8, 128, 128), BF16), vmem((8, 128, 128), BF16), vmem((4, 256, snps), BF16),
        vmem((2, UNIT, 256), BF16), vmem((2, UNIT, 256), BF16), vmem((2, UNIT, 256), BF16), vmem((2, UNIT, 256), BF16),
        vmem((2, 2, UNIT, 256), BF16), vmem((2, 4, UNIT, 128), BF16), vmem((2, 4, UNIT, 128), BF16),
        vmem((2, 4, UNIT, 128), F32), vmem((2, UNIT, 256), F32), vmem((2, UNIT, 128), BF16), vmem((2, UNIT, 128), BF16),
        vmem((2, UNIT, 128), BF16), vmem((2, UNIT, 128), BF16), vmem((2, UNIT, 128), BF16), vmem((2, UNIT, 128), BF16),
        vmem((2, 2, UNIT, 128), BF16), vmem((rows, rhs), BF16), vmem((2, 2, 128, 128), F32), vmem((16, 128, 128), F32),
        sem((6,)), sem((8,)), sem((6,)),
        sem((2, 2)), sem((2, 16)), sem((2, 2)), sem((2, 8)), sem((2, 8)), sem((2, 8)),
        sem((2, 4)), sem((2, 8)), sem((2, 8)), sem((2, 8)), sem((2, 2)), sem((2, 4)), sem((2, 8)), sem((2, 2)),
        sem((2, 2)), sem((2, 4)),
    ]
    trailing, solved, grm = pl.pallas_call(
        kernel,
        out_shape=(
            jax.ShapeDtypeStruct((blocks, per_row, rhs), F32),
            jax.ShapeDtypeStruct((2, 2, 128, 128), F32),
            jax.ShapeDtypeStruct((rows, rhs), BF16),
        ),
        in_specs=[pl.BlockSpec(memory_space=pltpu.SMEM)] + [anywhere] * 6,
        out_specs=(anywhere,) * 3,
        scratch_shapes=scratch,
        compiler_params=pltpu.CompilerParams(
            collective_id=0, has_side_effects=True, vmem_limit_bytes=56 * 1024 * 1024
        ),
        cost_estimate=pl.CostEstimate(flops=10_000_000_000, bytes_accessed=14_000_000, transcendentals=0),
    )(
        first_block, residual, diag_inverse, panels, probe_solved.reshape(rows, rhs),
        genotypes.reshape(rows, snps), annotation.reshape(16, 128),
    )
    return (
        trailing,
        solved.reshape(2, 256, 128),
        grm.reshape(blocks, per_row, 1, rhs),
    )


def solution(mesh):
    in_specs = (
        P(None, "row", None),
        P(None, "col", "row"),
        P(None, None, "row", "col"),
        P(),
        P(None, "row", None),
        P(None, "row", "col"),
        P("col"),
    )
    out_specs = (P(None, "row", None), P(None, "col", None), P(None, "row", "col", None))
    return jax.shard_map(shards, mesh=mesh, in_specs=in_specs, out_specs=out_specs, check_vma=False)
```

```python
import jax
import jax.numpy as jnp
from jax import lax
from jax.experimental import pallas as pl
from jax.experimental.pallas import tpu as pltpu
from jax.sharding import PartitionSpec as P

MESH = pl.DeviceIdType.MESH
F32 = jnp.float32
BF16 = jnp.bfloat16
SNPS = 16384
CHIPS = 8
COLS = 8
UNIT = 512


def dot(a, b):
    return jnp.dot(a, b, preferred_element_type=F32)


def dot_nt(a, b):
    return lax.dot_general(a, b, (((1,), (1,)), ((), ())), preferred_element_type=F32)


def kernel(
    first_ref, residual, diag, panels, probe, geno, annot,
    trail_v, sol_v, out_v,
    res_v, diag_v, pan_v, probe_v, pt_v, geno_v, ann_v,
    half_s, core_r, chip_r, full_s, full_r,
    u_s, u_x, u_r, t0_v, t_s, t_r, tx_s, tx_r, upd_v,
    lo_s, lo_r, lp_v, l_s, l_r, lf_v, lfo_v, w_v,
    za_s, za_r, zd_s, zc_s, zb_r, xs_s, xs_r, xown_v, c0_v, zx_s, zx_r,
    xa_s, xa_r, xd_s, xc_s, xb_r,
    in_sem, geno_sem,
    core_sem, chip_sem, full_sem, ux_sem, u_sem, t_sem, tx_sem, upd_sem,
    lo_sem, l_sem, lf_sem, lfo_sem, za_sem, zb_sem, xs_sem, zx_sem, xa_sem, xb_sem,
):
    row, col = lax.axis_index("row"), lax.axis_index("col")
    chip, core = lax.div(row, 2), lax.rem(row, 2)
    zpos, xhi = lax.div(col, 2), lax.rem(col, 2)

    def mate():
        return (chip * 2 + (1 - core), col)

    def chip_at(offset):
        return (lax.rem(chip + offset, CHIPS) * 2 + core, col)

    def z_at(offset):
        return (row, lax.rem(zpos + offset, 4) * 2 + xhi)

    def x_mate():
        return (row, zpos * 2 + (1 - xhi))

    pending = []

    def remote(src, dst, sems, index, to):
        return pltpu.make_async_remote_copy(
            src_ref=src, dst_ref=dst, send_sem=sems.at[0, index], recv_sem=sems.at[1, index],
            device_id=to, device_id_type=MESH,
        )

    def send(src, dst, sems, index, to):
        copy = remote(src, dst, sems, index, to)
        copy.start()
        pending.append(copy)

    def local(src, dst, sem):
        copy = pltpu.make_async_copy(src, dst, sem)
        copy.start()
        return copy

    barrier = pltpu.get_barrier_semaphore()
    for d in range(1, CHIPS):
        pl.semaphore_signal(barrier, inc=1, device_id=chip_at(d), device_id_type=MESH)
    for d in range(1, 4):
        pl.semaphore_signal(barrier, inc=1, device_id=z_at(d), device_id_type=MESH)
    pl.semaphore_signal(barrier, inc=1, device_id=x_mate(), device_id_type=MESH)
    pl.semaphore_signal(barrier, inc=1, device_id=mate(), device_id_type=MESH)

    c_probe = local(probe, probe_v, in_sem.at[2])
    c_geno = []
    for g in range(8):
        base = (1 - core) * 1024 if g < 4 else core * 1024
        start = pl.multiple_of(base + (g % 4) * 256, 256)
        c_geno.append(local(geno.at[:, pl.ds(start, 256)], geno_v.at[:, pl.ds(g * 256, 256)], geno_sem.at[g]))
    c_res = local(residual, res_v, in_sem.at[0])
    c_diag = local(diag, diag_v, in_sem.at[1])
    other8 = pl.multiple_of((1 - core) * 8, 8)
    own8 = pl.multiple_of(core * 8, 8)
    c_ann0 = local(annot.at[pl.ds(other8, 8)], ann_v.at[pl.ds(0, 8)], in_sem.at[4])
    c_ann1 = local(annot.at[pl.ds(own8, 8)], ann_v.at[pl.ds(8, 8)], in_sem.at[5])
    c_pan = local(panels, pan_v, in_sem.at[3])

    block = first_ref[0]

    def solve_begin(s, values):
        partial = dot(diag_v[s], values.astype(BF16))
        half_s[s, 0] = partial[:128]
        half_s[s, 1] = partial[128:]

    def solve_core(s):
        send(half_s.at[s, 1 - core], core_r.at[s], core_sem, s, mate())

    def solve_chips(s):
        remote(core_r.at[s], core_r.at[s], core_sem, s, mate()).wait_recv()
        chip_r[s, chip] = (half_s[s, core] + core_r[s]).astype(BF16)
        for d in range(1, CHIPS):
            send(chip_r.at[s, chip], chip_r.at[s, chip], chip_sem, s * 8 + d, chip_at(d))

    def solve_sum(s):
        for d in range(1, CHIPS):
            slot = lax.rem(chip + CHIPS - d, CHIPS)
            remote(chip_r.at[s, slot], chip_r.at[s, slot], chip_sem, s * 8 + d, chip_at(d)).wait_recv()
        total = chip_r[s, 0].astype(F32)
        for p in range(1, CHIPS):
            total = total + chip_r[s, p].astype(F32)
        full_s[s] = total
        send(full_s.at[s], full_r.at[s], full_sem, s, mate())

    def solve_end(s):
        remote(full_s.at[s], full_r.at[s], full_sem, s, mate()).wait_recv()
        sol_v[s, core] = full_s[s]
        sol_v[s, 1 - core] = full_r[s]
        return jnp.concatenate([sol_v[s, 0], sol_v[s, 1]], axis=0).astype(BF16)

    c_probe.wait()
    pt_v[...] = probe_v[...].T
    for g in range(4):
        c_geno[g].wait()
        lo_s[g] = dot(pt_v[...], geno_v[:, pl.ds(g * 256, 256)]).astype(BF16)
    for g in range(4):
        c_geno[4 + g].wait()
        lp_v[g] = dot(pt_v[...], geno_v[:, pl.ds((4 + g) * 256, 256)])
    c_res.wait()
    c_diag.wait()
    solve_begin(0, res_v[block])
    pl.semaphore_wait(barrier, 12)
    for g in range(4):
        send(lo_s.at[g], lo_r.at[g], lo_sem, g, mate())
    solve_core(0)
    for g in range(4):
        remote(lo_s.at[g], lo_r.at[g], lo_sem, g, mate()).wait_recv()
        part = (lp_v[g] + lo_r[g].astype(F32)).astype(BF16)
        for h in range(2):
            l_s[2 * g + h] = part[:, h * 128:(h + 1) * 128]
    for d in range(1, CHIPS):
        send(l_s.at[lax.rem(chip + d, CHIPS)], l_r.at[d], l_sem, d, chip_at(d))
    solve_chips(0)

    total = l_s[chip].astype(F32)
    for d in range(1, CHIPS):
        remote(l_s.at[0], l_r.at[d], l_sem, d, chip_at(d)).wait_recv()
        total = total + l_r[d].astype(F32)
    lf_v[chip] = (total * (1.0 / SNPS)).astype(BF16)
    for d in range(1, CHIPS):
        send(lf_v.at[chip], lf_v.at[chip], lf_sem, d, chip_at(d))
    send(lf_v.at[chip], lfo_v.at[chip], lfo_sem, 0, mate())

    solve_sum(0)
    c_ann0.wait()
    c_ann1.wait()
    c_pan.wait()
    solved0 = solve_end(0)
    u_s[...] = dot(pan_v[0, block + 1], solved0).astype(BF16)
    send(u_s, u_x, ux_sem, 0, x_mate())

    z_off = (2, 1, 3, 0)

    def build(half, chunk, value):
        ids = ann_v[pl.ds(half * 8 + chunk, 1), :]
        lanes = pl.ds(pl.multiple_of(half * 1024 + chunk * 128, 128), 128)
        for s in range(4):
            for side in range(2):
                owner = lax.rem(zpos + z_off[s], 4) * 2 + (xhi if side == 0 else 1 - xhi)
                mask = jnp.where(ids == owner, 1.0, 0.0).astype(BF16)
                w_v[s, side * 128:(side + 1) * 128, lanes] = value * mask

    build(1, chip, lf_v[chip])
    for d in range(1, CHIPS):
        slot = lax.rem(chip + CHIPS - d, CHIPS)
        remote(lf_v.at[slot], lf_v.at[slot], lf_sem, d, chip_at(d)).wait_recv()
        send(lf_v.at[slot], lfo_v.at[slot], lfo_sem, d, mate())
        build(1, slot, lf_v[slot])
    remote(u_s, u_x, ux_sem, 0, x_mate()).wait_recv()
    u_r[zpos] = (u_s[...].astype(F32) + u_x[...].astype(F32)).astype(BF16)
    for d in range(1, 4):
        send(u_r.at[zpos], u_r.at[zpos], u_sem, d, z_at(d))
    for d in range(CHIPS):
        slot = lax.rem(chip + CHIPS - d, CHIPS)
        remote(lf_v.at[slot], lfo_v.at[slot], lfo_sem, d, mate()).wait_recv()
        build(0, slot, lfo_v[slot])

    def unit(b, s):
        return dot_nt(geno_v[pl.ds(b * UNIT, UNIT), :], w_v[s])

    Z2, ZP, ZM, Z0 = 0, 1, 2, 3

    def x_first(b, s):
        value = unit(2 + b, s)
        xown_v[b, s] = value[:, :128]
        xs_s[b, s] = value[:, 128:].astype(BF16)
        send(xs_s.at[b, s], xs_r.at[b, s], xs_sem, b * 4 + s, x_mate())

    def x_arrived(b, s):
        remote(xs_s.at[b, s], xs_r.at[b, s], xs_sem, b * 4 + s, x_mate()).wait_recv()
        return xown_v[b, s] + xs_r[b, s].astype(F32)

    za_s[0] = unit(0, Z2).astype(BF16)
    send(za_s.at[0], za_r.at[0], za_sem, 0, z_at(1))
    x_first(0, Z2)
    za_s[1] = unit(1, Z2).astype(BF16)
    send(za_s.at[1], za_r.at[1], za_sem, 1, z_at(3))
    x_first(1, Z2)

    for d in range(1, 4):
        slot = lax.rem(zpos + 4 - d, 4)
        remote(u_r.at[slot], u_r.at[slot], u_sem, d, z_at(d)).wait_recv()
    u_total = u_r[0].astype(F32)
    for j in range(1, 4):
        u_total = u_total + u_r[j].astype(F32)
    solve_begin(1, res_v[block + 1] - u_total)
    solve_core(1)

    zd_s[0] = unit(1, ZP).astype(BF16)
    send(zd_s.at[0], zb_r.at[0, 1], zb_sem, 1, z_at(1))
    solve_chips(1)
    x_first(1, ZP)
    zd_s[1] = unit(0, ZM).astype(BF16)
    send(zd_s.at[1], zb_r.at[1, 0], zb_sem, 2, z_at(3))
    for j in range(16):
        keep = jnp.where(j > block, 1.0, 0.0).astype(F32)
        t0_v[j] = dot(pan_v[0, j], solved0) * keep
    x_first(0, ZM)

    value = unit(0, ZP)
    remote(za_s.at[0], za_r.at[0], za_sem, 0, z_at(1)).wait_recv()
    zc_s[0] = (value + za_r[0].astype(F32)).astype(BF16)
    send(zc_s.at[0], zb_r.at[0, 0], zb_sem, 0, z_at(1))
    solve_sum(1)
    x_first(0, ZP)
    value = unit(1, ZM)
    remote(za_s.at[1], za_r.at[1], za_sem, 1, z_at(3)).wait_recv()
    zc_s[1] = (value + za_r[1].astype(F32)).astype(BF16)
    send(zc_s.at[1], zb_r.at[1, 1], zb_sem, 3, z_at(3))

    solved1 = solve_end(1)
    for j in range(16):
        keep = jnp.where(j > block + 1, 1.0, 0.0).astype(F32)
        t_s[j // 4, j % 4] = (t0_v[j] + dot(pan_v[1, j], solved1) * keep).astype(BF16)
    for d in range(1, 4):
        send(t_s.at[lax.rem(zpos + d, 4)], t_r.at[d], t_sem, d, z_at(d))
    x_first(1, ZM)

    xa_s[0] = x_arrived(0, Z2).astype(BF16)
    send(xa_s.at[0], xa_r.at[0], xa_sem, 0, z_at(1))
    xa_s[1] = x_arrived(1, Z2).astype(BF16)
    send(xa_s.at[1], xa_r.at[1], xa_sem, 1, z_at(3))
    x_first(0, Z0)
    x_first(1, Z0)
    c0_v[0] = unit(0, Z0)
    c0_v[1] = unit(1, Z0)

    total = t_s[zpos].astype(F32)
    for d in range(1, 4):
        remote(t_s.at[0], t_r.at[d], t_sem, d, z_at(d)).wait_recv()
        total = total + t_r[d].astype(F32)
    tx_s[...] = total.astype(BF16)
    send(tx_s, tx_r, tx_sem, 0, x_mate())

    xd_s[0] = x_arrived(1, ZP).astype(BF16)
    send(xd_s.at[0], xb_r.at[0, 1], xb_sem, 1, z_at(1))
    xd_s[1] = x_arrived(0, ZM).astype(BF16)
    send(xd_s.at[1], xb_r.at[1, 0], xb_sem, 2, z_at(3))

    def z_arrived(b):
        for way in range(2):
            remote(zc_s.at[0], zb_r.at[way, b], zb_sem, way * 2 + b, z_at(1)).wait_recv()
        sums = c0_v[b] + zb_r[0, b].astype(F32) + zb_r[1, b].astype(F32)
        c0_v[b] = sums
        zx_s[b] = sums[:, 128:].astype(BF16)
        send(zx_s.at[b], zx_r.at[b], zx_sem, b, x_mate())

    z_arrived(0)
    z_arrived(1)

    remote(tx_s, tx_r, tx_sem, 0, x_mate()).wait_recv()
    upd_v[zpos] = (tx_s[...].astype(F32) + tx_r[...].astype(F32)).astype(BF16)
    for d in range(1, 4):
        send(upd_v.at[zpos], upd_v.at[zpos], upd_sem, d, z_at(d))

    value = x_arrived(0, ZP)
    remote(xa_s.at[0], xa_r.at[0], xa_sem, 0, z_at(1)).wait_recv()
    xc_s[0] = (value + xa_r[0].astype(F32)).astype(BF16)
    send(xc_s.at[0], xb_r.at[0, 0], xb_sem, 0, z_at(1))
    value = x_arrived(1, ZM)
    remote(xa_s.at[1], xa_r.at[1], xa_sem, 1, z_at(3)).wait_recv()
    xc_s[1] = (value + xa_r[1].astype(F32)).astype(BF16)
    send(xc_s.at[1], xb_r.at[1, 1], xb_sem, 3, z_at(3))

    for d in range(1, 4):
        slot = lax.rem(zpos + 4 - d, 4)
        remote(upd_v.at[slot], upd_v.at[slot], upd_sem, d, z_at(d)).wait_recv()
    for j in range(16):
        trail_v[j] = res_v[j] - upd_v[j // 4, j % 4].astype(F32)

    def emit(b, value):
        out_v[pl.ds(b * UNIT, UNIT), :] = value.astype(BF16)

    for b in range(2):
        remote(zx_s.at[b], zx_r.at[b], zx_sem, b, x_mate()).wait_recv()
        emit(b, c0_v[b, :, :128] + zx_r[b].astype(F32))
    for b in range(2):
        value = x_arrived(b, Z0)
        for way in range(2):
            remote(xc_s.at[0], xb_r.at[way, b], xb_sem, way * 2 + b, z_at(1)).wait_recv()
            value = value + xb_r[way, b].astype(F32)
        emit(2 + b, value)

    for copy in pending:
        copy.wait_send()


def store(trail_v, sol_v, out_v, trailing, solved, grm, sems):
    copies = [
        pltpu.make_async_copy(trail_v, trailing, sems.at[0]),
        pltpu.make_async_copy(sol_v, solved, sems.at[1]),
        pltpu.make_async_copy(out_v, grm, sems.at[2]),
    ]
    for copy in copies:
        copy.start()
    for copy in copies:
        copy.wait()


def shards(residual, diag_inverse, panels, first_block, probe_solved, genotypes, annotation):
    blocks, per_row, rhs = residual.shape
    rows = blocks * per_row
    snps = genotypes.shape[2]
    vmem = pltpu.VMEM
    sem = pltpu.SemaphoreType.DMA
    anywhere = pl.BlockSpec(memory_space=pl.ANY)
    in_vmem = pl.BlockSpec(memory_space=pltpu.VMEM)
    scratch = [
        vmem((16, 128, 128), F32), vmem((2, 256, 128), BF16), vmem((2, 16, 128, 256), BF16),
        vmem((rows, rhs), BF16), vmem((rhs, rows), BF16), vmem((rows, snps), BF16), vmem((16, 128), jnp.int32),
        vmem((2, 2, 128, 128), F32), vmem((2, 128, 128), F32), vmem((2, 8, 128, 128), BF16),
        vmem((2, 128, 128), F32), vmem((2, 128, 128), F32),
        vmem((128, 128), BF16), vmem((128, 128), BF16), vmem((4, 128, 128), BF16),
        vmem((16, 128, 128), F32), vmem((4, 4, 128, 128), BF16), vmem((4, 4, 128, 128), BF16),
        vmem((4, 128, 128), BF16), vmem((4, 128, 128), BF16), vmem((4, 4, 128, 128), BF16),
        vmem((4, 128, 256), BF16), vmem((4, 128, 256), BF16), vmem((4, 128, 256), F32),
        vmem((8, 128, 128), BF16), vmem((8, 128, 128), BF16),
        vmem((8, 128, 128), BF16), vmem((8, 128, 128), BF16), vmem((4, 256, snps), BF16),
        vmem((2, UNIT, 256), BF16), vmem((2, UNIT, 256), BF16), vmem((2, UNIT, 256), BF16), vmem((2, UNIT, 256), BF16),
        vmem((2, 2, UNIT, 256), BF16), vmem((2, 4, UNIT, 128), BF16), vmem((2, 4, UNIT, 128), BF16),
        vmem((2, 4, UNIT, 128), F32), vmem((2, UNIT, 256), F32), vmem((2, UNIT, 128), BF16), vmem((2, UNIT, 128), BF16),
        vmem((2, UNIT, 128), BF16), vmem((2, UNIT, 128), BF16), vmem((2, UNIT, 128), BF16), vmem((2, UNIT, 128), BF16),
        vmem((2, 2, UNIT, 128), BF16),
        sem((6,)), sem((8,)),
        sem((2, 2)), sem((2, 16)), sem((2, 2)), sem((2, 1)), sem((2, 4)), sem((2, 4)), sem((2, 1)), sem((2, 4)),
        sem((2, 4)), sem((2, 8)), sem((2, 8)), sem((2, 8)), sem((2, 2)), sem((2, 4)), sem((2, 8)), sem((2, 2)),
        sem((2, 2)), sem((2, 4)),
    ]
    results = (
        jax.ShapeDtypeStruct((blocks, per_row, rhs), F32),
        jax.ShapeDtypeStruct((2, 2, 128, 128), F32),
        jax.ShapeDtypeStruct((rows, rhs), BF16),
    )
    parts = pl.pallas_call(
        kernel,
        out_shape=tuple(pltpu.VMEM(r.shape, r.dtype) for r in results),
        in_specs=[pl.BlockSpec(memory_space=pltpu.SMEM)] + [pl.BlockSpec(memory_space=pltpu.HBM)] * 6,
        out_specs=(in_vmem,) * 3,
        scratch_shapes=scratch,
        compiler_params=pltpu.CompilerParams(
            collective_id=0, has_side_effects=True, vmem_limit_bytes=58 * 1024 * 1024
        ),
        cost_estimate=pl.CostEstimate(flops=10_000_000_000, bytes_accessed=14_000_000, transcendentals=0),
    )(
        first_block, residual, diag_inverse, panels, probe_solved.reshape(rows, rhs),
        genotypes.reshape(rows, snps), annotation.reshape(16, 128),
    )
    trailing, solved, grm = pl.pallas_call(
        store,
        out_shape=results,
        in_specs=[anywhere] * 3,
        out_specs=(anywhere,) * 3,
        scratch_shapes=[sem((3,))],
        compiler_params=pltpu.CompilerParams(vmem_limit_bytes=4 * 1024 * 1024),
    )(*parts)
    return (
        trailing,
        solved.reshape(2, 256, 128),
        grm.reshape(blocks, per_row, 1, rhs),
    )


def solution(mesh):
    in_specs = (
        P(None, "row", None),
        P(None, "col", "row"),
        P(None, None, "row", "col"),
        P(),
        P(None, "row", None),
        P(None, "row", "col"),
        P("col"),
    )
    out_specs = (P(None, "row", None), P(None, "col", None), P(None, "row", "col", None))
    return jax.shard_map(shards, mesh=mesh, in_specs=in_specs, out_specs=out_specs, check_vma=False)
```

```python
import jax
import jax.numpy as jnp
from jax import lax
from jax.experimental import pallas as pl
from jax.experimental.pallas import tpu as pltpu
from jax.sharding import PartitionSpec as P

MESH = pl.DeviceIdType.MESH
F32 = jnp.float32
BF16 = jnp.bfloat16
SNPS = 16384
CHIPS = 8
COLS = 8
ZROWS = 448
XROWS = 576


def dot(a, b):
    return jnp.dot(a, b, preferred_element_type=F32)


def dot_nt(a, b):
    return lax.dot_general(a, b, (((1,), (1,)), ((), ())), preferred_element_type=F32)


def kernel(
    first_ref, residual, diag, panels, probe, geno, annot,
    trail_v, sol_v, out_v,
    res_v, diag_v, pan_v, probe_v, pt_v, geno_v, ann_v,
    half_s, core_r, pair_s, pair_r, chip_r, full_s, full_r,
    u_s, u_x, u_r, t0_v, t_s, t_r, tx_s, tx_r, upd_v,
    lo_s, lo_r, lp_v, l_s, l_r, lf_v, lfo_v, w_v,
    za_s, za_r, zd_s, zc_s, zb_r, xs_s, xs_r, xown_v, c0_v, zx_s, zx_r,
    xa_s, xa_r, xd_s, xc_s, xb_r,
    first_v, in_sem, geno_sem,
    core_sem, pair_sem, chip_sem, full_sem, ux_sem, u_sem, t_sem, tx_sem, upd_sem,
    lo_sem, l_sem, lf_sem, lfo_sem, za_sem, zb_sem, xs_sem, zx_sem, xa_sem, xb_sem,
):
    row, col = lax.axis_index("row"), lax.axis_index("col")
    chip, core = lax.div(row, 2), lax.rem(row, 2)
    zpos, xhi = lax.div(col, 2), lax.rem(col, 2)
    ypos = lax.rem(chip, 4)

    def mate():
        return (chip * 2 + (1 - core), col)

    def chip_at(offset):
        return (lax.rem(chip + offset, CHIPS) * 2 + core, col)

    def y_at(offset):
        return ((lax.div(chip, 4) * 4 + lax.rem(ypos + offset, 4)) * 2 + core, col)

    def z_at(offset):
        return (row, lax.rem(zpos + offset, 4) * 2 + xhi)

    def x_mate():
        return (row, zpos * 2 + (1 - xhi))

    pending = []

    def remote(src, dst, sems, index, to):
        return pltpu.make_async_remote_copy(
            src_ref=src, dst_ref=dst, send_sem=sems.at[0, index], recv_sem=sems.at[1, index],
            device_id=to, device_id_type=MESH,
        )

    def send(src, dst, sems, index, to):
        copy = remote(src, dst, sems, index, to)
        copy.start()
        pending.append(copy)

    def local(src, dst, sem):
        copy = pltpu.make_async_copy(src, dst, sem)
        copy.start()
        return copy

    barrier = pltpu.get_barrier_semaphore()
    for d in range(1, CHIPS):
        pl.semaphore_signal(barrier, inc=1, device_id=chip_at(d), device_id_type=MESH)
    for d in range(1, 4):
        pl.semaphore_signal(barrier, inc=1, device_id=z_at(d), device_id_type=MESH)
    pl.semaphore_signal(barrier, inc=1, device_id=x_mate(), device_id_type=MESH)
    pl.semaphore_signal(barrier, inc=1, device_id=mate(), device_id_type=MESH)

    c_first = local(first_ref, first_v, in_sem.at[6])
    c_probe = local(probe, probe_v, in_sem.at[2])
    c_geno = []
    for g in range(8):
        base = (1 - core) * 1024 if g < 4 else core * 1024
        start = pl.multiple_of(base + (g % 4) * 256, 256)
        c_geno.append(local(geno.at[:, pl.ds(start, 256)], geno_v.at[:, pl.ds(g * 256, 256)], geno_sem.at[g]))
    c_res = local(residual, res_v, in_sem.at[0])
    c_diag = local(diag, diag_v, in_sem.at[1])
    other8 = pl.multiple_of((1 - core) * 8, 8)
    own8 = pl.multiple_of(core * 8, 8)
    c_ann0 = local(annot.at[pl.ds(other8, 8)], ann_v.at[pl.ds(0, 8)], in_sem.at[4])
    c_ann1 = local(annot.at[pl.ds(own8, 8)], ann_v.at[pl.ds(8, 8)], in_sem.at[5])
    c_pan = local(panels, pan_v, in_sem.at[3])

    c_first.wait()
    block = first_v[0]

    def solve_begin(s, values):
        partial = dot(diag_v[s], values.astype(BF16))
        half_s[s, 0] = partial[:128]
        half_s[s, 1] = partial[128:]

    def solve_core(s):
        send(half_s.at[s, 1 - core], core_r.at[s], core_sem, s, mate())

    def solve_pair(s):
        remote(core_r.at[s], core_r.at[s], core_sem, s, mate()).wait_recv()
        pair_s[s] = (half_s[s, core] + core_r[s]).astype(BF16)
        send(pair_s.at[s], pair_r.at[s], pair_sem, s, chip_at(4))

    def solve_y(s):
        remote(pair_s.at[s], pair_r.at[s], pair_sem, s, chip_at(4)).wait_recv()
        chip_r[s, ypos] = (pair_s[s].astype(F32) + pair_r[s].astype(F32)).astype(BF16)
        for d in range(1, 4):
            send(chip_r.at[s, ypos], chip_r.at[s, ypos], chip_sem, s * 4 + d, y_at(d))

    def solve_sum(s):
        for d in range(1, 4):
            slot = lax.rem(ypos + 4 - d, 4)
            remote(chip_r.at[s, slot], chip_r.at[s, slot], chip_sem, s * 4 + d, y_at(d)).wait_recv()
        total = chip_r[s, 0].astype(F32)
        for p in range(1, 4):
            total = total + chip_r[s, p].astype(F32)
        full_s[s] = total
        send(full_s.at[s], full_r.at[s], full_sem, s, mate())

    def solve_end(s):
        remote(full_s.at[s], full_r.at[s], full_sem, s, mate()).wait_recv()
        sol_v[s, core] = full_s[s]
        sol_v[s, 1 - core] = full_r[s]
        return jnp.concatenate([sol_v[s, 0], sol_v[s, 1]], axis=0).astype(BF16)

    c_probe.wait()
    pt_v[...] = probe_v[...].T
    for g in range(4):
        c_geno[g].wait()
        lo_s[g] = dot(pt_v[...], geno_v[:, pl.ds(g * 256, 256)]).astype(BF16)
    c_res.wait()
    c_diag.wait()
    solve_begin(0, res_v[block])
    pl.semaphore_wait(barrier, 12)
    solve_core(0)
    for g in range(4):
        send(lo_s.at[g], lo_r.at[g], lo_sem, g, mate())
    c_geno[4].wait()
    lp_v[0] = dot(pt_v[...], geno_v[:, pl.ds(1024, 256)])
    solve_pair(0)
    c_geno[5].wait()
    lp_v[1] = dot(pt_v[...], geno_v[:, pl.ds(1280, 256)])
    c_geno[6].wait()
    lp_v[2] = dot(pt_v[...], geno_v[:, pl.ds(1536, 256)])
    c_geno[7].wait()
    lp_v[3] = dot(pt_v[...], geno_v[:, pl.ds(1792, 256)])
    for g in range(4):
        remote(lo_s.at[g], lo_r.at[g], lo_sem, g, mate()).wait_recv()
        part = (lp_v[g] + lo_r[g].astype(F32)).astype(BF16)
        for h in range(2):
            p = 2 * g + h
            l_s[p] = part[:, h * 128:(h + 1) * 128]

            @pl.when(chip != p)
            def _():
                d = lax.rem(p + CHIPS - chip, CHIPS)
                remote(l_s.at[p], l_r.at[d], l_sem, d, (p * 2 + core, col)).start()

    solve_y(0)
    total = l_s[chip].astype(F32)
    for d in range(1, CHIPS):
        remote(l_s.at[0], l_r.at[d], l_sem, d, chip_at(d)).wait_recv()
        total = total + l_r[d].astype(F32)
    lf_v[chip] = (total * (1.0 / SNPS)).astype(BF16)
    for d in range(1, CHIPS):
        send(lf_v.at[chip], lf_v.at[chip], lf_sem, d, chip_at(d))
    send(lf_v.at[chip], lfo_v.at[chip], lfo_sem, 0, mate())

    solve_sum(0)
    c_ann0.wait()
    c_ann1.wait()
    c_pan.wait()
    solved0 = solve_end(0)
    u_s[...] = dot(pan_v[0, block + 1], solved0).astype(BF16)
    send(u_s, u_x, ux_sem, 0, x_mate())

    z_off = (2, 1, 3, 0)

    def build(half, chunk, value):
        ids = ann_v[pl.ds(half * 8 + chunk, 1), :]
        lanes = pl.ds(pl.multiple_of(half * 1024 + chunk * 128, 128), 128)
        for s in range(4):
            for side in range(2):
                owner = lax.rem(zpos + z_off[s], 4) * 2 + (xhi if side == 0 else 1 - xhi)
                mask = jnp.where(ids == owner, 1.0, 0.0).astype(BF16)
                w_v[s, side * 128:(side + 1) * 128, lanes] = value * mask

    build(1, chip, lf_v[chip])
    for d in range(1, CHIPS):
        slot = lax.rem(chip + CHIPS - d, CHIPS)
        remote(lf_v.at[slot], lf_v.at[slot], lf_sem, d, chip_at(d)).wait_recv()
        send(lf_v.at[slot], lfo_v.at[slot], lfo_sem, d, mate())
        build(1, slot, lf_v[slot])
    remote(u_s, u_x, ux_sem, 0, x_mate()).wait_recv()
    u_r[zpos] = (u_s[...].astype(F32) + u_x[...].astype(F32)).astype(BF16)
    for d in range(1, 4):
        send(u_r.at[zpos], u_r.at[zpos], u_sem, d, z_at(d))
    for d in range(CHIPS):
        slot = lax.rem(chip + CHIPS - d, CHIPS)
        remote(lf_v.at[slot], lfo_v.at[slot], lfo_sem, d, mate()).wait_recv()
        build(0, slot, lfo_v[slot])

    Z2, ZP, ZM, Z0 = 0, 1, 2, 3

    def z_unit(b, s):
        return dot_nt(geno_v[pl.ds(b * ZROWS, ZROWS), :], w_v[s])

    def xs(b, s):
        value = dot_nt(geno_v[pl.ds(2 * ZROWS + b * XROWS, XROWS), :], w_v[s])
        xown_v[b, s] = value[:, :128]
        xs_s[b, s] = value[:, 128:].astype(BF16)
        send(xs_s.at[b, s], xs_r.at[b, s], xs_sem, b * 4 + s, x_mate())

    def x_arrived(b, s):
        remote(xs_s.at[b, s], xs_r.at[b, s], xs_sem, b * 4 + s, x_mate()).wait_recv()
        return xown_v[b, s] + xs_r[b, s].astype(F32)

    WAY = (1, 3)
    NEAR = (ZP, ZM)

    def za(b):
        za_s[b] = z_unit(b, Z2).astype(BF16)
        send(za_s.at[b], za_r.at[b], za_sem, b, z_at(WAY[b]))

    def zd(b):
        zd_s[b] = z_unit(1 - b, NEAR[b]).astype(BF16)
        send(zd_s.at[b], zb_r.at[b, 1 - b], zb_sem, b * 2 + 1 - b, z_at(WAY[b]))

    def zc(b):
        value = z_unit(b, NEAR[b])
        remote(za_s.at[b], za_r.at[b], za_sem, b, z_at(WAY[b])).wait_recv()
        zc_s[b] = (value + za_r[b].astype(F32)).astype(BF16)
        send(zc_s.at[b], zb_r.at[b, b], zb_sem, b * 2 + b, z_at(WAY[b]))

    def z(b):
        c0_v[b] = z_unit(b, Z0)

    def zx(b):
        for way in range(2):
            remote(zc_s.at[0], zb_r.at[way, b], zb_sem, way * 2 + b, z_at(WAY[way])).wait_recv()
        sums = c0_v[b] + zb_r[0, b].astype(F32) + zb_r[1, b].astype(F32)
        c0_v[b] = sums
        zx_s[b] = sums[:, 128:].astype(BF16)
        send(zx_s.at[b], zx_r.at[b], zx_sem, b, x_mate())

    def xa(b):
        xa_s[b] = x_arrived(b, Z2).astype(BF16)
        send(xa_s.at[b], xa_r.at[b], xa_sem, b, z_at(WAY[b]))

    def xd(b):
        xd_s[b] = x_arrived(1 - b, NEAR[b]).astype(BF16)
        send(xd_s.at[b], xb_r.at[b, 1 - b], xb_sem, b * 2 + 1 - b, z_at(WAY[b]))

    def xc(b):
        value = x_arrived(b, NEAR[b])
        remote(xa_s.at[b], xa_r.at[b], xa_sem, b, z_at(WAY[b])).wait_recv()
        xc_s[b] = (value + xa_r[b].astype(F32)).astype(BF16)
        send(xc_s.at[b], xb_r.at[b, b], xb_sem, b * 2 + b, z_at(WAY[b]))

    def fz(b):
        remote(zx_s.at[b], zx_r.at[b], zx_sem, b, x_mate()).wait_recv()
        out_v[pl.ds(b * ZROWS, ZROWS), :] = (c0_v[b, :, :128] + zx_r[b].astype(F32)).astype(BF16)

    def fx(b):
        value = x_arrived(b, Z0)
        for way in range(2):
            remote(xc_s.at[0], xb_r.at[way, b], xb_sem, way * 2 + b, z_at(WAY[way])).wait_recv()
            value = value + xb_r[way, b].astype(F32)
        out_v[pl.ds(2 * ZROWS + b * XROWS, XROWS), :] = value.astype(BF16)

    def step_begin():
        for d in range(1, 4):
            slot = lax.rem(zpos + 4 - d, 4)
            remote(u_r.at[slot], u_r.at[slot], u_sem, d, z_at(d)).wait_recv()
        total = u_r[0].astype(F32)
        for j in range(1, 4):
            total = total + u_r[j].astype(F32)
        solve_begin(1, res_v[block + 1] - total)
        solve_core(1)

    def update_first():
        for j in range(16):
            keep = jnp.where(j > block, 1.0, 0.0).astype(F32)
            t0_v[j] = dot(pan_v[0, j], solved0) * keep

    def update_scatter():
        solved1 = solve_end(1)
        for j in range(16):
            keep = jnp.where(j > block + 1, 1.0, 0.0).astype(F32)
            t_s[j // 4, j % 4] = (t0_v[j] + dot(pan_v[1, j], solved1) * keep).astype(BF16)
        for d in range(1, 4):
            send(t_s.at[lax.rem(zpos + d, 4)], t_r.at[d], t_sem, d, z_at(d))

    def update_swap():
        total = t_s[zpos].astype(F32)
        for d in range(1, 4):
            remote(t_s.at[0], t_r.at[d], t_sem, d, z_at(d)).wait_recv()
            total = total + t_r[d].astype(F32)
        tx_s[...] = total.astype(BF16)
        send(tx_s, tx_r, tx_sem, 0, x_mate())

    def update_gather():
        remote(tx_s, tx_r, tx_sem, 0, x_mate()).wait_recv()
        upd_v[zpos] = (tx_s[...].astype(F32) + tx_r[...].astype(F32)).astype(BF16)
        for d in range(1, 4):
            send(upd_v.at[zpos], upd_v.at[zpos], upd_sem, d, z_at(d))

    def update_end():
        for d in range(1, 4):
            slot = lax.rem(zpos + 4 - d, 4)
            remote(upd_v.at[slot], upd_v.at[slot], upd_sem, d, z_at(d)).wait_recv()
        for j in range(16):
            trail_v[j] = res_v[j] - upd_v[j // 4, j % 4].astype(F32)

    za(0)
    za(1)
    xs(1, ZP)
    step_begin()
    zd(1)
    zd(0)
    solve_pair(1)
    xs(0, ZM)
    update_first()
    z(1)
    xs(1, Z2)
    zc(0)
    solve_y(1)
    zc(1)
    xs(0, Z2)
    xs(0, ZP)
    solve_sum(1)
    update_scatter()
    xa(1)
    xs(1, ZM)
    xa(0)
    z(0)
    xd(1)
    xd(0)
    xs(1, Z0)
    update_swap()
    xc(0)
    xc(1)
    zx(0)
    xs(0, Z0)
    update_gather()
    zx(1)
    fx(1)
    fx(0)
    fz(1)
    fz(0)
    update_end()

    for copy in pending:
        copy.wait_send()
    for d in range(1, CHIPS):
        remote(l_s.at[0], l_r.at[d], l_sem, d, chip_at(d)).wait_send()


def store(trail_v, sol_v, out_v, trailing, solved, grm, sems):
    copies = [
        pltpu.make_async_copy(trail_v, trailing, sems.at[0]),
        pltpu.make_async_copy(sol_v, solved, sems.at[1]),
        pltpu.make_async_copy(out_v, grm, sems.at[2]),
    ]
    for copy in copies:
        copy.start()
    for copy in copies:
        copy.wait()


def shards(residual, diag_inverse, panels, first_block, probe_solved, genotypes, annotation):
    blocks, per_row, rhs = residual.shape
    rows = blocks * per_row
    snps = genotypes.shape[2]
    vmem = pltpu.VMEM
    sem = pltpu.SemaphoreType.DMA
    anywhere = pl.BlockSpec(memory_space=pl.ANY)
    in_vmem = pl.BlockSpec(memory_space=pltpu.VMEM)
    scratch = [
        vmem((16, 128, 128), F32), vmem((2, 256, 128), BF16), vmem((2, 16, 128, 256), BF16),
        vmem((rows, rhs), BF16), vmem((rhs, rows), BF16), vmem((rows, snps), BF16), vmem((16, 128), jnp.int32),
        vmem((2, 2, 128, 128), F32), vmem((2, 128, 128), F32), vmem((2, 128, 128), BF16), vmem((2, 128, 128), BF16),
        vmem((2, 4, 128, 128), BF16),
        vmem((2, 128, 128), F32), vmem((2, 128, 128), F32),
        vmem((128, 128), BF16), vmem((128, 128), BF16), vmem((4, 128, 128), BF16),
        vmem((16, 128, 128), F32), vmem((4, 4, 128, 128), BF16), vmem((4, 4, 128, 128), BF16),
        vmem((4, 128, 128), BF16), vmem((4, 128, 128), BF16), vmem((4, 4, 128, 128), BF16),
        vmem((4, 128, 256), BF16), vmem((4, 128, 256), BF16), vmem((4, 128, 256), F32),
        vmem((8, 128, 128), BF16), vmem((8, 128, 128), BF16),
        vmem((8, 128, 128), BF16), vmem((8, 128, 128), BF16), vmem((4, 256, snps), BF16),
        vmem((2, ZROWS, 256), BF16), vmem((2, ZROWS, 256), BF16), vmem((2, ZROWS, 256), BF16), vmem((2, ZROWS, 256), BF16),
        vmem((2, 2, ZROWS, 256), BF16), vmem((2, 4, XROWS, 128), BF16), vmem((2, 4, XROWS, 128), BF16),
        vmem((2, 4, XROWS, 128), F32), vmem((2, ZROWS, 256), F32), vmem((2, ZROWS, 128), BF16), vmem((2, ZROWS, 128), BF16),
        vmem((2, XROWS, 128), BF16), vmem((2, XROWS, 128), BF16), vmem((2, XROWS, 128), BF16), vmem((2, XROWS, 128), BF16),
        vmem((2, 2, XROWS, 128), BF16),
        pltpu.SMEM((1,), jnp.int32), sem((7,)), sem((8,)),
        sem((2, 2)), sem((2, 2)), sem((2, 8)), sem((2, 2)), sem((2, 1)), sem((2, 4)), sem((2, 4)), sem((2, 1)), sem((2, 4)),
        sem((2, 4)), sem((2, 8)), sem((2, 8)), sem((2, 8)), sem((2, 2)), sem((2, 4)), sem((2, 8)), sem((2, 2)),
        sem((2, 2)), sem((2, 4)),
    ]
    results = (
        jax.ShapeDtypeStruct((blocks, per_row, rhs), F32),
        jax.ShapeDtypeStruct((2, 2, 128, 128), F32),
        jax.ShapeDtypeStruct((rows, rhs), BF16),
    )
    parts = pl.pallas_call(
        kernel,
        out_shape=tuple(pltpu.VMEM(r.shape, r.dtype) for r in results),
        in_specs=[anywhere] * 7,
        out_specs=(in_vmem,) * 3,
        scratch_shapes=scratch,
        compiler_params=pltpu.CompilerParams(
            collective_id=0, has_side_effects=True, vmem_limit_bytes=58 * 1024 * 1024
        ),
        cost_estimate=pl.CostEstimate(flops=10_000_000_000, bytes_accessed=14_000_000, transcendentals=0),
    )(
        first_block, residual, diag_inverse, panels, probe_solved.reshape(rows, rhs),
        genotypes.reshape(rows, snps), annotation.reshape(16, 128),
    )
    trailing, solved, grm = pl.pallas_call(
        store,
        out_shape=results,
        in_specs=[anywhere] * 3,
        out_specs=(anywhere,) * 3,
        scratch_shapes=[sem((3,))],
        compiler_params=pltpu.CompilerParams(vmem_limit_bytes=4 * 1024 * 1024),
    )(*parts)
    return (
        trailing,
        solved.reshape(2, 256, 128),
        grm.reshape(blocks, per_row, 1, rhs),
    )


def solution(mesh):
    in_specs = (
        P(None, "row", None),
        P(None, "col", "row"),
        P(None, None, "row", "col"),
        P(),
        P(None, "row", None),
        P(None, "row", "col"),
        P("col"),
    )
    out_specs = (P(None, "row", None), P(None, "col", None), P(None, "row", "col", None))
    return jax.shard_map(shards, mesh=mesh, in_specs=in_specs, out_specs=out_specs, check_vma=False)
```

```python
import jax
import jax.numpy as jnp
from jax import lax
from jax.experimental import pallas as pl
from jax.experimental.pallas import tpu as pltpu
from jax.sharding import PartitionSpec as P

MESH = pl.DeviceIdType.MESH
F32 = jnp.float32
BF16 = jnp.bfloat16
SNPS = 16384
CHIPS = 8
FAR_FIRST = (6, 5, 7, 2, 4, 1, 3)
COLS = 8
ZROWS = 528
XROWS = 496


def dot(a, b):
    return jnp.dot(a, b, preferred_element_type=F32)


def dot_nt(a, b):
    return lax.dot_general(a, b, (((1,), (1,)), ((), ())), preferred_element_type=F32)


def kernel(
    first_ref, residual, diag, panels, probe, geno, annot,
    trail_v, sol_v, out_v,
    res_v, diag_v, pan_v, probe_v, pt_v, geno_v, ann_v,
    half_s, core_r, pair_s, pair_r, chip_r, full_s, full_r,
    u_s, u_x, u_r, t0_v, t_s, t_r, tx_s, tx_r, upd_v,
    lo_s, lo_r, lp_v, l_s, l_r, lf_v, lfo_v, w_v,
    za_s, za_r, zd_s, zc_s, zb_r, xs_s, xs_r, xown_v, c0_v, zx_s, zx_r,
    xa_s, xa_r, xd_s, xc_s, xb_r,
    first_v, in_sem, geno_sem,
    core_sem, pair_sem, chip_sem, full_sem, ux_sem, u_sem, t_sem, tx_sem, upd_sem,
    lo_sem, l_sem, lf_sem, lfo_sem, za_sem, zb_sem, xs_sem, zx_sem, xa_sem, xb_sem,
):
    row, col = lax.axis_index("row"), lax.axis_index("col")
    chip, core = lax.div(row, 2), lax.rem(row, 2)
    zpos, xhi = lax.div(col, 2), lax.rem(col, 2)
    xpos, ypos = lax.div(chip, 4), lax.rem(chip, 4)

    def mate():
        return (chip * 2 + (1 - core), col)

    def chip_up(offset):
        return lax.rem(xpos + offset // 4, 2) * 4 + lax.rem(ypos + offset % 4, 4)

    def chip_down(offset):
        return lax.rem(xpos + offset // 4, 2) * 4 + lax.rem(ypos + 4 - offset % 4, 4)

    def chip_at(offset):
        return (chip_up(offset) * 2 + core, col)

    def y_at(offset):
        return ((lax.div(chip, 4) * 4 + lax.rem(ypos + offset, 4)) * 2 + core, col)

    def z_at(offset):
        return (row, lax.rem(zpos + offset, 4) * 2 + xhi)

    def x_mate():
        return (row, zpos * 2 + (1 - xhi))

    pending = []

    def remote(src, dst, sems, index, to):
        return pltpu.make_async_remote_copy(
            src_ref=src, dst_ref=dst, send_sem=sems.at[0, index], recv_sem=sems.at[1, index],
            device_id=to, device_id_type=MESH,
        )

    def send(src, dst, sems, index, to):
        copy = remote(src, dst, sems, index, to)
        copy.start()
        pending.append(copy)

    def local(src, dst, sem):
        copy = pltpu.make_async_copy(src, dst, sem)
        copy.start()
        return copy

    barrier = pltpu.get_barrier_semaphore()
    for d in range(1, CHIPS):
        pl.semaphore_signal(barrier, inc=1, device_id=chip_at(d), device_id_type=MESH)
    for d in range(1, 4):
        pl.semaphore_signal(barrier, inc=1, device_id=z_at(d), device_id_type=MESH)
    pl.semaphore_signal(barrier, inc=1, device_id=x_mate(), device_id_type=MESH)
    pl.semaphore_signal(barrier, inc=1, device_id=mate(), device_id_type=MESH)

    c_first = local(first_ref, first_v, in_sem.at[6])
    c_probe = local(probe, probe_v, in_sem.at[2])
    c_geno = []
    for g in range(8):
        base = (1 - core) * 1024 if g < 4 else core * 1024
        start = pl.multiple_of(base + (g % 4) * 256, 256)
        c_geno.append(local(geno.at[:, pl.ds(start, 256)], geno_v.at[:, pl.ds(g * 256, 256)], geno_sem.at[g]))
    c_res = local(residual, res_v, in_sem.at[0])
    c_diag = local(diag, diag_v, in_sem.at[1])
    other8 = pl.multiple_of((1 - core) * 8, 8)
    own8 = pl.multiple_of(core * 8, 8)
    c_ann0 = local(annot.at[pl.ds(other8, 8)], ann_v.at[pl.ds(0, 8)], in_sem.at[4])
    c_ann1 = local(annot.at[pl.ds(own8, 8)], ann_v.at[pl.ds(8, 8)], in_sem.at[5])
    c_pan = local(panels, pan_v, in_sem.at[3])

    c_first.wait()
    block = first_v[0]

    def solve_begin(s, values):
        partial = dot(diag_v[s], values.astype(BF16))
        half_s[s, 0] = partial[:128]
        half_s[s, 1] = partial[128:]

    def solve_core(s):
        send(half_s.at[s, 1 - core], core_r.at[s], core_sem, s, mate())

    def solve_pair(s):
        remote(core_r.at[s], core_r.at[s], core_sem, s, mate()).wait_recv()
        pair_s[s] = (half_s[s, core] + core_r[s]).astype(BF16)
        send(pair_s.at[s], pair_r.at[s], pair_sem, s, chip_at(4))

    def solve_y(s):
        remote(pair_s.at[s], pair_r.at[s], pair_sem, s, chip_at(4)).wait_recv()
        chip_r[s, ypos] = (pair_s[s].astype(F32) + pair_r[s].astype(F32)).astype(BF16)
        for d in range(1, 4):
            send(chip_r.at[s, ypos], chip_r.at[s, ypos], chip_sem, s * 4 + d, y_at(d))

    def solve_sum(s):
        for d in range(1, 4):
            slot = lax.rem(ypos + 4 - d, 4)
            remote(chip_r.at[s, slot], chip_r.at[s, slot], chip_sem, s * 4 + d, y_at(d)).wait_recv()
        total = chip_r[s, 0].astype(F32)
        for p in range(1, 4):
            total = total + chip_r[s, p].astype(F32)
        full_s[s] = total
        send(full_s.at[s], full_r.at[s], full_sem, s, mate())

    def solve_end(s):
        remote(full_s.at[s], full_r.at[s], full_sem, s, mate()).wait_recv()
        sol_v[s, core] = full_s[s]
        sol_v[s, 1 - core] = full_r[s]
        return jnp.concatenate([sol_v[s, 0], sol_v[s, 1]], axis=0).astype(BF16)

    c_probe.wait()
    pt_v[...] = probe_v[...].T
    for g in range(4):
        c_geno[g].wait()
        lo_s[g] = dot(pt_v[...], geno_v[:, pl.ds(g * 256, 256)]).astype(BF16)
    c_res.wait()
    c_diag.wait()
    solve_begin(0, res_v[block])
    pl.semaphore_wait(barrier, 12)
    solve_core(0)
    for g in range(4):
        send(lo_s.at[g], lo_r.at[g], lo_sem, g, mate())
    c_geno[4].wait()
    lp_v[0] = dot(pt_v[...], geno_v[:, pl.ds(1024, 256)])
    solve_pair(0)
    c_geno[5].wait()
    lp_v[1] = dot(pt_v[...], geno_v[:, pl.ds(1280, 256)])
    c_geno[6].wait()
    lp_v[2] = dot(pt_v[...], geno_v[:, pl.ds(1536, 256)])
    c_geno[7].wait()
    lp_v[3] = dot(pt_v[...], geno_v[:, pl.ds(1792, 256)])
    for g in range(4):
        remote(lo_s.at[g], lo_r.at[g], lo_sem, g, mate()).wait_recv()
        part = (lp_v[g] + lo_r[g].astype(F32)).astype(BF16)
        for h in range(2):
            l_s[2 * g + h] = part[:, h * 128:(h + 1) * 128]
    for d in FAR_FIRST:
        send(l_s.at[chip_up(d)], l_r.at[d], l_sem, d, chip_at(d))

    solve_y(0)
    total = l_s[chip].astype(F32)
    for d in reversed(FAR_FIRST):
        remote(l_s.at[0], l_r.at[d], l_sem, d, chip_at(d)).wait_recv()
        total = total + l_r[d].astype(F32)
    lf_v[chip] = (total * (1.0 / SNPS)).astype(BF16)
    for d in FAR_FIRST:
        send(lf_v.at[chip], lf_v.at[chip], lf_sem, d, chip_at(d))
    send(lf_v.at[chip], lfo_v.at[chip], lfo_sem, 0, mate())

    solve_sum(0)
    c_ann0.wait()
    c_ann1.wait()
    c_pan.wait()
    solved0 = solve_end(0)
    u_s[...] = dot(pan_v[0, block + 1], solved0).astype(BF16)
    send(u_s, u_x, ux_sem, 0, x_mate())

    z_off = (2, 1, 3, 0)

    def build(half, chunk, value):
        ids = ann_v[pl.ds(half * 8 + chunk, 1), :]
        lanes = pl.ds(pl.multiple_of(half * 1024 + chunk * 128, 128), 128)
        for s in range(4):
            for side in range(2):
                owner = lax.rem(zpos + z_off[s], 4) * 2 + (xhi if side == 0 else 1 - xhi)
                mask = jnp.where(ids == owner, 1.0, 0.0).astype(BF16)
                w_v[s, side * 128:(side + 1) * 128, lanes] = value * mask

    build(1, chip, lf_v[chip])
    for d in reversed(FAR_FIRST):
        slot = chip_down(d)
        remote(lf_v.at[slot], lf_v.at[slot], lf_sem, d, chip_at(d)).wait_recv()
        send(lf_v.at[slot], lfo_v.at[slot], lfo_sem, d, mate())
        build(1, slot, lf_v[slot])
    remote(u_s, u_x, ux_sem, 0, x_mate()).wait_recv()
    u_r[zpos] = (u_s[...].astype(F32) + u_x[...].astype(F32)).astype(BF16)
    for d in range(1, 4):
        send(u_r.at[zpos], u_r.at[zpos], u_sem, d, z_at(d))
    for d in (0,) + FAR_FIRST[::-1]:
        slot = chip_down(d)
        remote(lf_v.at[slot], lfo_v.at[slot], lfo_sem, d, mate()).wait_recv()
        build(0, slot, lfo_v[slot])

    Z2, ZP, ZM, Z0 = 0, 1, 2, 3

    def z_unit(b, s):
        return dot_nt(geno_v[pl.ds(b * ZROWS, ZROWS), :], w_v[s])

    def xs(b, s):
        value = dot_nt(geno_v[pl.ds(2 * ZROWS + b * XROWS, XROWS), :], w_v[s])
        xown_v[b, s] = value[:, :128]
        xs_s[b, s] = value[:, 128:].astype(BF16)
        send(xs_s.at[b, s], xs_r.at[b, s], xs_sem, b * 4 + s, x_mate())

    def x_arrived(b, s):
        remote(xs_s.at[b, s], xs_r.at[b, s], xs_sem, b * 4 + s, x_mate()).wait_recv()
        return xown_v[b, s] + xs_r[b, s].astype(F32)

    WAY = (1, 3)
    NEAR = (ZP, ZM)

    def za(b):
        za_s[b] = z_unit(b, Z2).astype(BF16)
        send(za_s.at[b], za_r.at[b], za_sem, b, z_at(WAY[b]))

    def zd(b):
        zd_s[b] = z_unit(1 - b, NEAR[b]).astype(BF16)
        send(zd_s.at[b], zb_r.at[b, 1 - b], zb_sem, b * 2 + 1 - b, z_at(WAY[b]))

    def zc(b):
        value = z_unit(b, NEAR[b])
        remote(za_s.at[b], za_r.at[b], za_sem, b, z_at(WAY[b])).wait_recv()
        zc_s[b] = (value + za_r[b].astype(F32)).astype(BF16)
        send(zc_s.at[b], zb_r.at[b, b], zb_sem, b * 2 + b, z_at(WAY[b]))

    def z(b):
        c0_v[b] = z_unit(b, Z0)

    def zx(b):
        for way in range(2):
            remote(zc_s.at[0], zb_r.at[way, b], zb_sem, way * 2 + b, z_at(WAY[way])).wait_recv()
        sums = c0_v[b] + zb_r[0, b].astype(F32) + zb_r[1, b].astype(F32)
        c0_v[b] = sums
        zx_s[b] = sums[:, 128:].astype(BF16)
        send(zx_s.at[b], zx_r.at[b], zx_sem, b, x_mate())

    def xa(b):
        xa_s[b] = x_arrived(b, Z2).astype(BF16)
        send(xa_s.at[b], xa_r.at[b], xa_sem, b, z_at(WAY[b]))

    def xd(b):
        xd_s[b] = x_arrived(1 - b, NEAR[b]).astype(BF16)
        send(xd_s.at[b], xb_r.at[b, 1 - b], xb_sem, b * 2 + 1 - b, z_at(WAY[b]))

    def xc(b):
        value = x_arrived(b, NEAR[b])
        remote(xa_s.at[b], xa_r.at[b], xa_sem, b, z_at(WAY[b])).wait_recv()
        xc_s[b] = (value + xa_r[b].astype(F32)).astype(BF16)
        send(xc_s.at[b], xb_r.at[b, b], xb_sem, b * 2 + b, z_at(WAY[b]))

    def fz(b):
        remote(zx_s.at[b], zx_r.at[b], zx_sem, b, x_mate()).wait_recv()
        out_v[pl.ds(b * ZROWS, ZROWS), :] = (c0_v[b, :, :128] + zx_r[b].astype(F32)).astype(BF16)

    def fx(b):
        value = x_arrived(b, Z0)
        for way in range(2):
            remote(xc_s.at[0], xb_r.at[way, b], xb_sem, way * 2 + b, z_at(WAY[way])).wait_recv()
            value = value + xb_r[way, b].astype(F32)
        out_v[pl.ds(2 * ZROWS + b * XROWS, XROWS), :] = value.astype(BF16)

    def step_begin():
        for d in range(1, 4):
            slot = lax.rem(zpos + 4 - d, 4)
            remote(u_r.at[slot], u_r.at[slot], u_sem, d, z_at(d)).wait_recv()
        total = u_r[0].astype(F32)
        for j in range(1, 4):
            total = total + u_r[j].astype(F32)
        solve_begin(1, res_v[block + 1] - total)
        solve_core(1)

    def update_first():
        for j in range(16):
            keep = jnp.where(j > block, 1.0, 0.0).astype(F32)
            t0_v[j] = dot(pan_v[0, j], solved0) * keep

    def update_scatter():
        solved1 = solve_end(1)
        for j in range(16):
            keep = jnp.where(j > block + 1, 1.0, 0.0).astype(F32)
            t_s[j // 4, j % 4] = (t0_v[j] + dot(pan_v[1, j], solved1) * keep).astype(BF16)
        far, up, down = (lax.rem(zpos + d, 4) for d in (2, 1, 3))
        send(t_s.at[far, pl.ds(0, 2)], t_r.at[0, pl.ds(0, 2)], t_sem, 0, z_at(1))
        send(t_s.at[far, pl.ds(2, 2)], t_r.at[0, pl.ds(2, 2)], t_sem, 1, z_at(3))
        send(t_s.at[up, pl.ds(2, 2)], t_r.at[1, pl.ds(2, 2)], t_sem, 2, z_at(1))
        send(t_s.at[down, pl.ds(0, 2)], t_r.at[2, pl.ds(0, 2)], t_sem, 3, z_at(3))

    def update_relay():
        for way, near, part in ((0, lax.rem(zpos + 1, 4), 0), (1, lax.rem(zpos + 3, 4), 2)):
            rows = pl.ds(part, 2)
            remote(t_s.at[near, rows], t_r.at[0, rows], t_sem, way, z_at(WAY[way])).wait_recv()
            t_s[near, rows] = (t_s[near, rows].astype(F32) + t_r[0, rows].astype(F32)).astype(BF16)
            send(t_s.at[near, rows], t_r.at[1 + way, rows], t_sem, 4 + way, z_at(WAY[way]))

    def update_swap():
        for way, early, late in ((0, 2, 0), (1, 0, 2)):
            remote(t_s.at[0, pl.ds(early, 2)], t_r.at[1 + way, pl.ds(early, 2)], t_sem, 2 + way, z_at(WAY[way])).wait_recv()
            remote(t_s.at[0, pl.ds(late, 2)], t_r.at[1 + way, pl.ds(late, 2)], t_sem, 4 + way, z_at(WAY[way])).wait_recv()
        tx_s[...] = (t_s[zpos].astype(F32) + t_r[1].astype(F32) + t_r[2].astype(F32)).astype(BF16)
        send(tx_s, tx_r, tx_sem, 0, x_mate())

    def update_gather():
        remote(tx_s, tx_r, tx_sem, 0, x_mate()).wait_recv()
        upd_v[zpos] = (tx_s[...].astype(F32) + tx_r[...].astype(F32)).astype(BF16)
        for way in range(2):
            send(upd_v.at[zpos], upd_v.at[zpos], upd_sem, way, z_at(WAY[way]))

    def update_pass():
        for way, slot, part in ((0, lax.rem(zpos + 3, 4), 0), (1, lax.rem(zpos + 1, 4), 2)):
            rows = pl.ds(part, 2)
            remote(upd_v.at[slot], upd_v.at[slot], upd_sem, way, z_at(WAY[way])).wait_recv()
            send(upd_v.at[slot, rows], upd_v.at[slot, rows], upd_sem, 2 + way, z_at(WAY[way]))

    def update_end():
        far = lax.rem(zpos + 2, 4)
        for way, part in ((0, 0), (1, 2)):
            rows = pl.ds(part, 2)
            remote(upd_v.at[far, rows], upd_v.at[far, rows], upd_sem, 2 + way, z_at(WAY[way])).wait_recv()
        for j in range(16):
            trail_v[j] = res_v[j] - upd_v[j // 4, j % 4].astype(F32)

    za(0)
    za(1)
    step_begin()
    update_first()
    zd(1)
    solve_pair(1)
    xs(0, ZM)
    zd(0)
    xs(1, ZP)
    solve_y(1)
    xs(1, Z2)
    solve_sum(1)
    xs(1, ZM)
    xs(0, Z2)
    update_scatter()
    xd(1)
    xd(0)
    xs(1, Z0)
    xs(0, ZP)
    update_relay()
    zc(1)
    zc(0)
    update_swap()
    xs(0, Z0)
    z(1)
    xa(0)
    z(0)
    xa(1)
    update_gather()
    zx(0)
    xc(1)
    zx(1)
    xc(0)
    update_pass()
    fz(1)
    fz(0)
    fx(1)
    fx(0)
    update_end()

    for copy in pending:
        copy.wait_send()


def store(trail_v, sol_v, out_v, trailing, solved, grm, sems):
    copies = [
        pltpu.make_async_copy(trail_v, trailing, sems.at[0]),
        pltpu.make_async_copy(sol_v, solved, sems.at[1]),
        pltpu.make_async_copy(out_v, grm, sems.at[2]),
    ]
    for copy in copies:
        copy.start()
    for copy in copies:
        copy.wait()


def shards(residual, diag_inverse, panels, first_block, probe_solved, genotypes, annotation):
    blocks, per_row, rhs = residual.shape
    rows = blocks * per_row
    snps = genotypes.shape[2]
    vmem = pltpu.VMEM
    sem = pltpu.SemaphoreType.DMA
    anywhere = pl.BlockSpec(memory_space=pl.ANY)
    in_vmem = pl.BlockSpec(memory_space=pltpu.VMEM)
    scratch = [
        vmem((16, 128, 128), F32), vmem((2, 256, 128), BF16), vmem((2, 16, 128, 256), BF16),
        vmem((rows, rhs), BF16), vmem((rhs, rows), BF16), vmem((rows, snps), BF16), vmem((16, 128), jnp.int32),
        vmem((2, 2, 128, 128), F32), vmem((2, 128, 128), F32), vmem((2, 128, 128), BF16), vmem((2, 128, 128), BF16),
        vmem((2, 4, 128, 128), BF16),
        vmem((2, 128, 128), F32), vmem((2, 128, 128), F32),
        vmem((128, 128), BF16), vmem((128, 128), BF16), vmem((4, 128, 128), BF16),
        vmem((16, 128, 128), F32), vmem((4, 4, 128, 128), BF16), vmem((4, 4, 128, 128), BF16),
        vmem((4, 128, 128), BF16), vmem((4, 128, 128), BF16), vmem((4, 4, 128, 128), BF16),
        vmem((4, 128, 256), BF16), vmem((4, 128, 256), BF16), vmem((4, 128, 256), F32),
        vmem((8, 128, 128), BF16), vmem((8, 128, 128), BF16),
        vmem((8, 128, 128), BF16), vmem((8, 128, 128), BF16), vmem((4, 256, snps), BF16),
        vmem((2, ZROWS, 256), BF16), vmem((2, ZROWS, 256), BF16), vmem((2, ZROWS, 256), BF16), vmem((2, ZROWS, 256), BF16),
        vmem((2, 2, ZROWS, 256), BF16), vmem((2, 4, XROWS, 128), BF16), vmem((2, 4, XROWS, 128), BF16),
        vmem((2, 4, XROWS, 128), F32), vmem((2, ZROWS, 256), F32), vmem((2, ZROWS, 128), BF16), vmem((2, ZROWS, 128), BF16),
        vmem((2, XROWS, 128), BF16), vmem((2, XROWS, 128), BF16), vmem((2, XROWS, 128), BF16), vmem((2, XROWS, 128), BF16),
        vmem((2, 2, XROWS, 128), BF16),
        pltpu.SMEM((1,), jnp.int32), sem((7,)), sem((8,)),
        sem((2, 2)), sem((2, 2)), sem((2, 8)), sem((2, 2)), sem((2, 1)), sem((2, 4)), sem((2, 6)), sem((2, 1)), sem((2, 4)),
        sem((2, 4)), sem((2, 8)), sem((2, 8)), sem((2, 8)), sem((2, 2)), sem((2, 4)), sem((2, 8)), sem((2, 2)),
        sem((2, 2)), sem((2, 4)),
    ]
    results = (
        jax.ShapeDtypeStruct((blocks, per_row, rhs), F32),
        jax.ShapeDtypeStruct((2, 2, 128, 128), F32),
        jax.ShapeDtypeStruct((rows, rhs), BF16),
    )
    parts = pl.pallas_call(
        kernel,
        out_shape=tuple(pltpu.VMEM(r.shape, r.dtype) for r in results),
        in_specs=[anywhere] * 7,
        out_specs=(in_vmem,) * 3,
        scratch_shapes=scratch,
        compiler_params=pltpu.CompilerParams(
            collective_id=0, has_side_effects=True, vmem_limit_bytes=58 * 1024 * 1024
        ),
        cost_estimate=pl.CostEstimate(flops=10_000_000_000, bytes_accessed=14_000_000, transcendentals=0),
    )(
        first_block, residual, diag_inverse, panels, probe_solved.reshape(rows, rhs),
        genotypes.reshape(rows, snps), annotation.reshape(16, 128),
    )
    trailing, solved, grm = pl.pallas_call(
        store,
        out_shape=results,
        in_specs=[anywhere] * 3,
        out_specs=(anywhere,) * 3,
        scratch_shapes=[sem((3,))],
        compiler_params=pltpu.CompilerParams(vmem_limit_bytes=4 * 1024 * 1024),
    )(*parts)
    return (
        trailing,
        solved.reshape(2, 256, 128),
        grm.reshape(blocks, per_row, 1, rhs),
    )


def solution(mesh):
    in_specs = (
        P(None, "row", None),
        P(None, "col", "row"),
        P(None, None, "row", "col"),
        P(),
        P(None, "row", None),
        P(None, "row", "col"),
        P("col"),
    )
    out_specs = (P(None, "row", None), P(None, "col", None), P(None, "row", "col", None))
    return jax.shard_map(shards, mesh=mesh, in_specs=in_specs, out_specs=out_specs, check_vma=False)
```

```python
import jax
import jax.numpy as jnp
from jax import lax
from jax.experimental import pallas as pl
from jax.experimental.pallas import tpu as pltpu
from jax.sharding import PartitionSpec as P

MESH = pl.DeviceIdType.MESH
F32 = jnp.float32
BF16 = jnp.bfloat16
SNPS = 16384
CHIPS = 8
FAR_FIRST = (6, 5, 7, 2, 4, 1, 3)
COLS = 8
ZROWS = 528
XROWS = 496


def dot(a, b):
    return jnp.dot(a, b, preferred_element_type=F32)


def dot_nt(a, b):
    return lax.dot_general(a, b, (((1,), (1,)), ((), ())), preferred_element_type=F32)


def kernel(
    first_ref, residual, diag, panels, probe, geno, annot,
    trail_v, sol_v, out_v,
    res_v, diag_v, pan_v, probe_v, pt_v, geno_v, ann_v,
    half_s, core_r, pair_s, pair_r, chip_r, full_s, full_r,
    u_s, u_x, u_r, t0_v, t_s, t_r, tx_s, tx_r, upd_v,
    lo_s, lo_r, lp_v, l_s, l_r, lf_v, lfo_v, w_v,
    za_s, za_r, zd_s, zc_s, zb_r, xs_s, xs_r, xown_v, c0_v, zx_s, zx_r,
    xa_s, xa_r, xd_s, xc_s, xb_r,
    first_v, in_sem, geno_sem,
    core_sem, pair_sem, chip_sem, full_sem, ux_sem, u_sem, t_sem, tx_sem, upd_sem,
    lo_sem, l_sem, lf_sem, lfo_sem, za_sem, zb_sem, xs_sem, zx_sem, xa_sem, xb_sem,
):
    row, col = lax.axis_index("row"), lax.axis_index("col")
    chip, core = lax.div(row, 2), lax.rem(row, 2)
    zpos, xhi = lax.div(col, 2), lax.rem(col, 2)
    xpos, ypos = lax.div(chip, 4), lax.rem(chip, 4)

    def mate():
        return (chip * 2 + (1 - core), col)

    def chip_up(offset):
        return lax.rem(xpos + offset // 4, 2) * 4 + lax.rem(ypos + offset % 4, 4)

    def chip_down(offset):
        return lax.rem(xpos + offset // 4, 2) * 4 + lax.rem(ypos + 4 - offset % 4, 4)

    def chip_at(offset):
        return (chip_up(offset) * 2 + core, col)

    def y_at(offset):
        return ((lax.div(chip, 4) * 4 + lax.rem(ypos + offset, 4)) * 2 + core, col)

    def z_at(offset):
        return (row, lax.rem(zpos + offset, 4) * 2 + xhi)

    def x_mate():
        return (row, zpos * 2 + (1 - xhi))

    pending = []

    def remote(src, dst, sems, index, to):
        return pltpu.make_async_remote_copy(
            src_ref=src, dst_ref=dst, send_sem=sems.at[0, index], recv_sem=sems.at[1, index],
            device_id=to, device_id_type=MESH,
        )

    def send(src, dst, sems, index, to):
        copy = remote(src, dst, sems, index, to)
        copy.start()
        pending.append(copy)

    def local(src, dst, sem):
        copy = pltpu.make_async_copy(src, dst, sem)
        copy.start()
        return copy

    barrier = pltpu.get_barrier_semaphore()
    for d in FAR_FIRST:
        pl.semaphore_signal(barrier, inc=1, device_id=chip_at(d), device_id_type=MESH)
    for d in range(1, 4):
        pl.semaphore_signal(barrier, inc=1, device_id=z_at(d), device_id_type=MESH)
    pl.semaphore_signal(barrier, inc=1, device_id=x_mate(), device_id_type=MESH)
    pl.semaphore_signal(barrier, inc=1, device_id=mate(), device_id_type=MESH)

    c_first = local(first_ref, first_v, in_sem.at[6])
    c_probe = local(probe, probe_v, in_sem.at[2])
    c_geno = []
    for g in range(8):
        base = (1 - core) * 1024 if g < 4 else core * 1024
        start = pl.multiple_of(base + (g % 4) * 256, 256)
        c_geno.append(local(geno.at[:, pl.ds(start, 256)], geno_v.at[:, pl.ds(g * 256, 256)], geno_sem.at[g]))
    c_res = local(residual, res_v, in_sem.at[0])
    c_diag = local(diag, diag_v, in_sem.at[1])
    other8 = pl.multiple_of((1 - core) * 8, 8)
    own8 = pl.multiple_of(core * 8, 8)
    c_ann0 = local(annot.at[pl.ds(other8, 8)], ann_v.at[pl.ds(0, 8)], in_sem.at[4])
    c_ann1 = local(annot.at[pl.ds(own8, 8)], ann_v.at[pl.ds(8, 8)], in_sem.at[5])
    c_pan = local(panels, pan_v, in_sem.at[3])

    c_first.wait()
    block = first_v[0]

    def solve_begin(s, values):
        partial = dot(diag_v[s], values.astype(BF16))
        half_s[s, 0] = partial[:128]
        half_s[s, 1] = partial[128:]

    def solve_core(s):
        send(half_s.at[s, 1 - core], core_r.at[s], core_sem, s, mate())

    def solve_pair(s):
        remote(core_r.at[s], core_r.at[s], core_sem, s, mate()).wait_recv()
        pair_s[s] = (half_s[s, core] + core_r[s]).astype(BF16)
        send(pair_s.at[s], pair_r.at[s], pair_sem, s, chip_at(4))

    def solve_y(s):
        remote(pair_s.at[s], pair_r.at[s], pair_sem, s, chip_at(4)).wait_recv()
        chip_r[s, ypos] = (pair_s[s].astype(F32) + pair_r[s].astype(F32)).astype(BF16)
        for d in range(1, 4):
            send(chip_r.at[s, ypos], chip_r.at[s, ypos], chip_sem, s * 4 + d, y_at(d))

    def solve_sum(s):
        for d in range(1, 4):
            slot = lax.rem(ypos + 4 - d, 4)
            remote(chip_r.at[s, slot], chip_r.at[s, slot], chip_sem, s * 4 + d, y_at(d)).wait_recv()
        total = chip_r[s, 0].astype(F32)
        for p in range(1, 4):
            total = total + chip_r[s, p].astype(F32)
        full_s[s] = total
        send(full_s.at[s], full_r.at[s], full_sem, s, mate())

    def solve_end(s):
        remote(full_s.at[s], full_r.at[s], full_sem, s, mate()).wait_recv()
        sol_v[s, core] = full_s[s]
        sol_v[s, 1 - core] = full_r[s]
        return jnp.concatenate([sol_v[s, 0], sol_v[s, 1]], axis=0).astype(BF16)

    c_probe.wait()
    pt_v[...] = probe_v[...].T
    for g in range(4):
        c_geno[g].wait()
        lo_s[g] = dot(pt_v[...], geno_v[:, pl.ds(g * 256, 256)]).astype(BF16)
    c_res.wait()
    c_diag.wait()
    solve_begin(0, res_v[block])
    pl.semaphore_wait(barrier, 12)
    solve_core(0)
    for g in range(4):
        send(lo_s.at[g], lo_r.at[g], lo_sem, g, mate())
    c_geno[4].wait()
    lp_v[0] = dot(pt_v[...], geno_v[:, pl.ds(1024, 256)])
    solve_pair(0)
    c_geno[5].wait()
    lp_v[1] = dot(pt_v[...], geno_v[:, pl.ds(1280, 256)])
    c_geno[6].wait()
    lp_v[2] = dot(pt_v[...], geno_v[:, pl.ds(1536, 256)])
    c_geno[7].wait()
    lp_v[3] = dot(pt_v[...], geno_v[:, pl.ds(1792, 256)])
    for g in range(4):
        remote(lo_s.at[g], lo_r.at[g], lo_sem, g, mate()).wait_recv()
        part = (lp_v[g] + lo_r[g].astype(F32)).astype(BF16)
        for h in range(2):
            l_s[2 * g + h] = part[:, h * 128:(h + 1) * 128]
    for d in FAR_FIRST:
        send(l_s.at[chip_up(d)], l_r.at[d], l_sem, d, chip_at(d))

    solve_y(0)
    total = l_s[chip].astype(F32)
    for d in reversed(FAR_FIRST):
        remote(l_s.at[0], l_r.at[d], l_sem, d, chip_at(d)).wait_recv()
        total = total + l_r[d].astype(F32)
    lf_v[chip] = (total * (1.0 / SNPS)).astype(BF16)
    for d in FAR_FIRST:
        send(lf_v.at[chip], lf_v.at[chip], lf_sem, d, chip_at(d))
    send(lf_v.at[chip], lfo_v.at[chip], lfo_sem, 0, mate())

    solve_sum(0)
    c_ann0.wait()
    c_ann1.wait()
    c_pan.wait()
    solved0 = solve_end(0)
    u_s[...] = dot(pan_v[0, block + 1], solved0).astype(BF16)
    send(u_s, u_x, ux_sem, 0, x_mate())

    z_off = (2, 1, 3, 0)

    def build(half, chunk, value):
        ids = ann_v[pl.ds(half * 8 + chunk, 1), :]
        lanes = pl.ds(pl.multiple_of(half * 1024 + chunk * 128, 128), 128)
        for s in range(4):
            for side in range(2):
                owner = lax.rem(zpos + z_off[s], 4) * 2 + (xhi if side == 0 else 1 - xhi)
                mask = jnp.where(ids == owner, 1.0, 0.0).astype(BF16)
                w_v[s, side * 128:(side + 1) * 128, lanes] = value * mask

    build(1, chip, lf_v[chip])
    for d in reversed(FAR_FIRST):
        slot = chip_down(d)
        remote(lf_v.at[slot], lf_v.at[slot], lf_sem, d, chip_at(d)).wait_recv()
        send(lf_v.at[slot], lfo_v.at[slot], lfo_sem, d, mate())
        build(1, slot, lf_v[slot])
    remote(u_s, u_x, ux_sem, 0, x_mate()).wait_recv()
    u_r[zpos] = (u_s[...].astype(F32) + u_x[...].astype(F32)).astype(BF16)
    for d in range(1, 4):
        send(u_r.at[zpos], u_r.at[zpos], u_sem, d, z_at(d))
    for d in (0,) + FAR_FIRST[::-1]:
        slot = chip_down(d)
        remote(lf_v.at[slot], lfo_v.at[slot], lfo_sem, d, mate()).wait_recv()
        build(0, slot, lfo_v[slot])

    Z2, ZP, ZM, Z0 = 0, 1, 2, 3

    def z_unit(b, s):
        return dot_nt(geno_v[pl.ds(b * ZROWS, ZROWS), :], w_v[s])

    def xs(b, s):
        value = dot_nt(geno_v[pl.ds(2 * ZROWS + b * XROWS, XROWS), :], w_v[s])
        xown_v[b, s] = value[:, :128]
        xs_s[b, s] = value[:, 128:].astype(BF16)
        send(xs_s.at[b, s], xs_r.at[b, s], xs_sem, b * 4 + s, x_mate())

    def x_arrived(b, s):
        remote(xs_s.at[b, s], xs_r.at[b, s], xs_sem, b * 4 + s, x_mate()).wait_recv()
        return xown_v[b, s] + xs_r[b, s].astype(F32)

    WAY = (1, 3)
    NEAR = (ZP, ZM)

    def za(b):
        za_s[b] = z_unit(b, Z2).astype(BF16)
        send(za_s.at[b], za_r.at[b], za_sem, b, z_at(WAY[b]))

    def zd(b):
        zd_s[b] = z_unit(1 - b, NEAR[b]).astype(BF16)
        send(zd_s.at[b], zb_r.at[b, 1 - b], zb_sem, b * 2 + 1 - b, z_at(WAY[b]))

    def zc(b):
        value = z_unit(b, NEAR[b])
        remote(za_s.at[b], za_r.at[b], za_sem, b, z_at(WAY[b])).wait_recv()
        zc_s[b] = (value + za_r[b].astype(F32)).astype(BF16)
        send(zc_s.at[b], zb_r.at[b, b], zb_sem, b * 2 + b, z_at(WAY[b]))

    def z(b):
        c0_v[b] = z_unit(b, Z0)

    def zx(b):
        for way in range(2):
            remote(zc_s.at[0], zb_r.at[way, b], zb_sem, way * 2 + b, z_at(WAY[way])).wait_recv()
        sums = c0_v[b] + zb_r[0, b].astype(F32) + zb_r[1, b].astype(F32)
        c0_v[b] = sums
        zx_s[b] = sums[:, 128:].astype(BF16)
        send(zx_s.at[b], zx_r.at[b], zx_sem, b, x_mate())

    def xa(b):
        xa_s[b] = x_arrived(b, Z2).astype(BF16)
        send(xa_s.at[b], xa_r.at[b], xa_sem, b, z_at(WAY[b]))

    def xd(b):
        xd_s[b] = x_arrived(1 - b, NEAR[b]).astype(BF16)
        send(xd_s.at[b], xb_r.at[b, 1 - b], xb_sem, b * 2 + 1 - b, z_at(WAY[b]))

    def xc(b):
        value = x_arrived(b, NEAR[b])
        remote(xa_s.at[b], xa_r.at[b], xa_sem, b, z_at(WAY[b])).wait_recv()
        xc_s[b] = (value + xa_r[b].astype(F32)).astype(BF16)
        send(xc_s.at[b], xb_r.at[b, b], xb_sem, b * 2 + b, z_at(WAY[b]))

    def fz(b):
        remote(zx_s.at[b], zx_r.at[b], zx_sem, b, x_mate()).wait_recv()
        out_v[pl.ds(b * ZROWS, ZROWS), :] = (c0_v[b, :, :128] + zx_r[b].astype(F32)).astype(BF16)

    def fx(b):
        value = x_arrived(b, Z0)
        for way in range(2):
            remote(xc_s.at[0], xb_r.at[way, b], xb_sem, way * 2 + b, z_at(WAY[way])).wait_recv()
            value = value + xb_r[way, b].astype(F32)
        out_v[pl.ds(2 * ZROWS + b * XROWS, XROWS), :] = value.astype(BF16)

    def step_begin():
        for d in range(1, 4):
            slot = lax.rem(zpos + 4 - d, 4)
            remote(u_r.at[slot], u_r.at[slot], u_sem, d, z_at(d)).wait_recv()
        total = u_r[0].astype(F32)
        for j in range(1, 4):
            total = total + u_r[j].astype(F32)
        solve_begin(1, res_v[block + 1] - total)
        solve_core(1)

    def update_first():
        for j in range(16):
            keep = jnp.where(j > block, 1.0, 0.0).astype(F32)
            t0_v[j] = dot(pan_v[0, j], solved0) * keep

    def update_scatter():
        solved1 = solve_end(1)
        for j in range(16):
            keep = jnp.where(j > block + 1, 1.0, 0.0).astype(F32)
            t_s[j // 4, j % 4] = (t0_v[j] + dot(pan_v[1, j], solved1) * keep).astype(BF16)
        far, up, down = (lax.rem(zpos + d, 4) for d in (2, 1, 3))
        send(t_s.at[far, pl.ds(0, 2)], t_r.at[0, pl.ds(0, 2)], t_sem, 0, z_at(1))
        send(t_s.at[far, pl.ds(2, 2)], t_r.at[0, pl.ds(2, 2)], t_sem, 1, z_at(3))
        send(t_s.at[up, pl.ds(2, 2)], t_r.at[1, pl.ds(2, 2)], t_sem, 2, z_at(1))
        send(t_s.at[down, pl.ds(0, 2)], t_r.at[2, pl.ds(0, 2)], t_sem, 3, z_at(3))

    def update_relay():
        for way, near, part in ((0, lax.rem(zpos + 1, 4), 0), (1, lax.rem(zpos + 3, 4), 2)):
            rows = pl.ds(part, 2)
            remote(t_s.at[near, rows], t_r.at[0, rows], t_sem, way, z_at(WAY[way])).wait_recv()
            t_s[near, rows] = (t_s[near, rows].astype(F32) + t_r[0, rows].astype(F32)).astype(BF16)
            send(t_s.at[near, rows], t_r.at[1 + way, rows], t_sem, 4 + way, z_at(WAY[way]))

    def update_swap():
        for way, early, late in ((0, 2, 0), (1, 0, 2)):
            remote(t_s.at[0, pl.ds(early, 2)], t_r.at[1 + way, pl.ds(early, 2)], t_sem, 2 + way, z_at(WAY[way])).wait_recv()
            remote(t_s.at[0, pl.ds(late, 2)], t_r.at[1 + way, pl.ds(late, 2)], t_sem, 4 + way, z_at(WAY[way])).wait_recv()
        tx_s[...] = (t_s[zpos].astype(F32) + t_r[1].astype(F32) + t_r[2].astype(F32)).astype(BF16)
        send(tx_s, tx_r, tx_sem, 0, x_mate())

    def update_gather():
        remote(tx_s, tx_r, tx_sem, 0, x_mate()).wait_recv()
        upd_v[zpos] = (tx_s[...].astype(F32) + tx_r[...].astype(F32)).astype(BF16)
        for way in range(2):
            send(upd_v.at[zpos], upd_v.at[zpos], upd_sem, way, z_at(WAY[way]))

    def update_pass():
        for way, slot, part in ((0, lax.rem(zpos + 3, 4), 0), (1, lax.rem(zpos + 1, 4), 2)):
            rows = pl.ds(part, 2)
            remote(upd_v.at[slot], upd_v.at[slot], upd_sem, way, z_at(WAY[way])).wait_recv()
            send(upd_v.at[slot, rows], upd_v.at[slot, rows], upd_sem, 2 + way, z_at(WAY[way]))

    def update_end():
        far = lax.rem(zpos + 2, 4)
        for way, part in ((0, 0), (1, 2)):
            rows = pl.ds(part, 2)
            remote(upd_v.at[far, rows], upd_v.at[far, rows], upd_sem, 2 + way, z_at(WAY[way])).wait_recv()
        for j in range(16):
            trail_v[j] = res_v[j] - upd_v[j // 4, j % 4].astype(F32)

    za(0)
    za(1)
    step_begin()
    update_first()
    zd(1)
    solve_pair(1)
    xs(0, ZM)
    zd(0)
    xs(1, ZP)
    solve_y(1)
    xs(1, Z2)
    solve_sum(1)
    xs(1, ZM)
    xs(0, Z2)
    update_scatter()
    xd(1)
    xd(0)
    xs(1, Z0)
    xs(0, ZP)
    update_relay()
    zc(1)
    zc(0)
    update_swap()
    xs(0, Z0)
    z(1)
    xa(0)
    z(0)
    xa(1)
    update_gather()
    zx(0)
    xc(1)
    zx(1)
    xc(0)
    update_pass()
    fz(1)
    fz(0)
    fx(1)
    fx(0)
    update_end()

    for copy in pending:
        copy.wait_send()


def store(trail_v, sol_v, out_v, trailing, solved, grm, sems):
    copies = [
        pltpu.make_async_copy(trail_v.at[pl.ds(4 * j, 4)], trailing.at[pl.ds(4 * j, 4)], sems.at[j]) for j in range(4)
    ] + [
        pltpu.make_async_copy(out_v.at[pl.ds(1024 * j, 1024)], grm.at[pl.ds(1024 * j, 1024)], sems.at[4 + j])
        for j in range(2)
    ] + [pltpu.make_async_copy(sol_v, solved, sems.at[6])]
    for copy in copies:
        copy.start()
    for copy in copies:
        copy.wait()


def shards(residual, diag_inverse, panels, first_block, probe_solved, genotypes, annotation):
    blocks, per_row, rhs = residual.shape
    rows = blocks * per_row
    snps = genotypes.shape[2]
    vmem = pltpu.VMEM
    sem = pltpu.SemaphoreType.DMA
    anywhere = pl.BlockSpec(memory_space=pl.ANY)
    in_vmem = pl.BlockSpec(memory_space=pltpu.VMEM)
    scratch = [
        vmem((16, 128, 128), F32), vmem((2, 256, 128), BF16), vmem((2, 16, 128, 256), BF16),
        vmem((rows, rhs), BF16), vmem((rhs, rows), BF16), vmem((rows, snps), BF16), vmem((16, 128), jnp.int32),
        vmem((2, 2, 128, 128), F32), vmem((2, 128, 128), F32), vmem((2, 128, 128), BF16), vmem((2, 128, 128), BF16),
        vmem((2, 4, 128, 128), BF16),
        vmem((2, 128, 128), F32), vmem((2, 128, 128), F32),
        vmem((128, 128), BF16), vmem((128, 128), BF16), vmem((4, 128, 128), BF16),
        vmem((16, 128, 128), F32), vmem((4, 4, 128, 128), BF16), vmem((4, 4, 128, 128), BF16),
        vmem((4, 128, 128), BF16), vmem((4, 128, 128), BF16), vmem((4, 4, 128, 128), BF16),
        vmem((4, 128, 256), BF16), vmem((4, 128, 256), BF16), vmem((4, 128, 256), F32),
        vmem((8, 128, 128), BF16), vmem((8, 128, 128), BF16),
        vmem((8, 128, 128), BF16), vmem((8, 128, 128), BF16), vmem((4, 256, snps), BF16),
        vmem((2, ZROWS, 256), BF16), vmem((2, ZROWS, 256), BF16), vmem((2, ZROWS, 256), BF16), vmem((2, ZROWS, 256), BF16),
        vmem((2, 2, ZROWS, 256), BF16), vmem((2, 4, XROWS, 128), BF16), vmem((2, 4, XROWS, 128), BF16),
        vmem((2, 4, XROWS, 128), F32), vmem((2, ZROWS, 256), F32), vmem((2, ZROWS, 128), BF16), vmem((2, ZROWS, 128), BF16),
        vmem((2, XROWS, 128), BF16), vmem((2, XROWS, 128), BF16), vmem((2, XROWS, 128), BF16), vmem((2, XROWS, 128), BF16),
        vmem((2, 2, XROWS, 128), BF16),
        pltpu.SMEM((1,), jnp.int32), sem((7,)), sem((8,)),
        sem((2, 2)), sem((2, 2)), sem((2, 8)), sem((2, 2)), sem((2, 1)), sem((2, 4)), sem((2, 6)), sem((2, 1)), sem((2, 4)),
        sem((2, 4)), sem((2, 8)), sem((2, 8)), sem((2, 8)), sem((2, 2)), sem((2, 4)), sem((2, 8)), sem((2, 2)),
        sem((2, 2)), sem((2, 4)),
    ]
    results = (
        jax.ShapeDtypeStruct((blocks, per_row, rhs), F32),
        jax.ShapeDtypeStruct((2, 2, 128, 128), F32),
        jax.ShapeDtypeStruct((rows, rhs), BF16),
    )
    parts = pl.pallas_call(
        kernel,
        out_shape=tuple(pltpu.VMEM(r.shape, r.dtype) for r in results),
        in_specs=[anywhere] * 7,
        out_specs=(in_vmem,) * 3,
        scratch_shapes=scratch,
        compiler_params=pltpu.CompilerParams(
            collective_id=0, has_side_effects=True, vmem_limit_bytes=58 * 1024 * 1024
        ),
        cost_estimate=pl.CostEstimate(flops=10_000_000_000, bytes_accessed=14_000_000, transcendentals=0),
    )(
        first_block, residual, diag_inverse, panels, probe_solved.reshape(rows, rhs),
        genotypes.reshape(rows, snps), annotation.reshape(16, 128),
    )
    trailing, solved, grm = pl.pallas_call(
        store,
        out_shape=results,
        in_specs=[anywhere] * 3,
        out_specs=(anywhere,) * 3,
        scratch_shapes=[sem((7,))],
        compiler_params=pltpu.CompilerParams(vmem_limit_bytes=4 * 1024 * 1024),
    )(*parts)
    return (
        trailing,
        solved.reshape(2, 256, 128),
        grm.reshape(blocks, per_row, 1, rhs),
    )


def solution(mesh):
    in_specs = (
        P(None, "row", None),
        P(None, "col", "row"),
        P(None, None, "row", "col"),
        P(),
        P(None, "row", None),
        P(None, "row", "col"),
        P("col"),
    )
    out_specs = (P(None, "row", None), P(None, "col", None), P(None, "row", "col", None))
    return jax.shard_map(shards, mesh=mesh, in_specs=in_specs, out_specs=out_specs, check_vma=False)
```
